512 devices in a mesh: img: 32 (over z, core), bal: 16 (over y, x).
Axes of the slice: x: 4, y: 4, z: 16, core: 2. Of those that a mesh axis runs over, the one named last changes fastest.
Arguments:
- latent: bfloat16 [384, 192, 512], P('img', 'bal'), may hold values from -6 to 6
- gn_mean: float32 [32], replicated, may hold values from -1.5 to 1.5
- gn_rstd: float32 [32], replicated, may hold values from 0.5 to 2
- gn_gain: float32 [512], replicated, may hold values from 0.5 to 1.5
- gn_shift: float32 [512], replicated, may hold values from -3 to 3
- conv1_kernel: bfloat16 [3, 3, 512, 512], replicated, may hold values from -0.09375 to 0.09375
- conv1_bias: float32 [512], replicated, may hold values from -3 to 3
- conv2_kernel: bfloat16 [3, 3, 512, 512], replicated, may hold values from -0.09375 to 0.09375
- conv2_bias: float32 [512], replicated, may hold values from -3 to 3
- tile_dest: int32 [128, 64], P('img', 'bal'), may hold values from -1 to 127, as said below
Outputs:
- decoded: bfloat16 [768, 384, 512], P('img', 'bal')
The draws below stay inside these ranges and needn't reach their ends.
Inputs may be any that keep to these rules, and one draw needn't show every extreme that they name: `tile_dest`: tile (i, j) belongs to the device at img index i // 4 and bal index j // 4. A value d * 8 + s names the bal index d, within the same img index, that computes the tile, and its slot s there. Among the tiles of one img index every pair (d, s) is named by exactly one tile, so every device computes exactly 8 tiles. No device names one bal index d for more than 1 of its tiles; in every band one device has all its tiles active and names every bal index for exactly 1 of them.
All inputs are finite; a program needn't handle non-finite values.
Results may differ from the reference program's by a relative error of at most 0.0055.
Values may be sent and summed in bfloat16 or wider, within the bound.
No kernel may reach another device: no remote copies, remote signals or barrier semaphores. Data moves between devices by JAX's collectives and lax.ppermute only.
A program may use at most 64 MiB of HBM per device.

```python
import math
import jax
import jax.numpy as jnp
from jax import lax

C = 512
G = 32
TS = 3
TR = 4
TC = 4
SLOTS = 8
TILES_R = 128
TILES_C = 64
HEIGHT = 384
WIDTH = 192


def plan_tiles(key):
    bal_size = TILES_C // TC
    tile_count = TR * TC
    bands = TILES_R // TR
    total_tiles = bal_size * tile_count
    active_count = bal_size * SLOTS

    def one_band(band_key):
        key_fav, key_perm, key_order, key_dest = jax.random.split(band_key, 4)
        favored = jax.random.randint(key_fav, (), 0, bal_size)
        scores = jax.random.permutation(key_perm, total_tiles).astype(jnp.int32)
        owner_dev = jnp.arange(total_tiles, dtype=jnp.int32) // tile_count
        scores = jnp.where(owner_dev == favored, scores - total_tiles, scores)
        order = jnp.argsort(scores)
        position = jnp.argsort(order).astype(jnp.int32)
        active = position < active_count
        second = jax.random.permutation(key_order, total_tiles).astype(jnp.int32)
        sort_key = jnp.where(active, owner_dev * total_tiles + second, total_tiles * total_tiles + jnp.arange(total_tiles, dtype=jnp.int32))
        rank = jnp.argsort(jnp.argsort(sort_key)).astype(jnp.int32)
        dest_perm = jax.random.permutation(key_dest, bal_size).astype(jnp.int32)
        dest = dest_perm[rank % bal_size]
        return jnp.where(active, dest * SLOTS + rank // bal_size, -1)
    tile_codes = jax.vmap(one_band)(jax.random.split(key, bands))
    tile_codes = tile_codes.reshape(bands, bal_size, TR, TC).transpose(0, 2, 1, 3)
    return tile_codes.reshape(TILES_R, TILES_C).astype(jnp.int32)


def draw_tile_dest(key, part):
    key = jax.random.fold_in(key, 7)
    return plan_tiles(key)


def block_levels(rng, shape, cuts, least, top_value):
    loudness, own = 1.0, jax.random.fold_in(rng, 6)
    for dim, blocks in cuts:
        heights = jnp.exp(jax.random.uniform(jax.random.fold_in(own, dim), (blocks,), jnp.float32, least / len(cuts), top_value / len(cuts)))
        loudness = loudness * jnp.repeat(heights, shape[dim] // blocks).reshape([-1 if axis == dim else 1 for axis in range(len(shape))])
    return loudness


def scatter_about(stream_key, shape, scale, bound, shards=(), held_as=jnp.bfloat16):
    gain = block_levels(stream_key, shape, shards, -0.22, 0.18) if shards else 1.0
    values = jax.random.normal(stream_key, shape, jnp.float32) * scale * gain
    return jnp.minimum(jnp.maximum(values, -bound), bound).astype(held_as)


def setup_inputs(seed: int = 0) -> dict:
    arg_keys = jax.random.split(jax.random.key(seed), 11)
    latent = scatter_about(arg_keys[0], (HEIGHT, WIDTH, C), 1.0, 6.0, ((0, 32), (1, 16)))
    gn_mean = scatter_about(arg_keys[1], (G,), 0.3, 1.5, (), jnp.float32)
    gn_rstd = jnp.clip(jnp.exp(jax.random.uniform(arg_keys[2], (G,), jnp.float32, math.log(0.5), math.log(2.0))), 0.5, 2.0)
    gn_gain = jnp.clip(1.0 + 0.1 * jax.random.normal(arg_keys[3], (C,), jnp.float32), 0.5, 1.5)
    gn_shift = scatter_about(arg_keys[4], (C,), 0.5, 3.0, (), jnp.float32)
    conv1_kernel = scatter_about(arg_keys[5], (3, 3, C, C), (9 * C) ** -0.5, 0.09375)
    conv1_bias = scatter_about(arg_keys[6], (C,), 0.5, 3.0, (), jnp.float32)
    conv2_kernel = scatter_about(arg_keys[7], (3, 3, C, C), (9 * C) ** -0.5, 0.09375)
    conv2_bias = scatter_about(arg_keys[8], (C,), 0.5, 3.0, (), jnp.float32)
    tile_dest = draw_tile_dest(jax.random.fold_in(arg_keys[10], 71), 0)
    return {"latent": latent, "gn_mean": gn_mean, "gn_rstd": gn_rstd, "gn_gain": gn_gain, "gn_shift": gn_shift, "conv1_kernel": conv1_kernel, "conv1_bias": conv1_bias, "conv2_kernel": conv2_kernel, "conv2_bias": conv2_bias, "tile_dest": tile_dest}


def norm_act(latent, gn_mean, gn_rstd, gn_gain, gn_shift):
    per_group = latent.shape[-1] // gn_mean.shape[0]
    mean_full = jnp.repeat(gn_mean, per_group)
    rstd_full = jnp.repeat(gn_rstd, per_group)
    normed = (latent.astype(jnp.float32) - mean_full) * rstd_full * gn_gain + gn_shift
    return jax.nn.silu(normed).astype(jnp.bfloat16)


def conv_three(region, kernel, bias_vec):
    batch_count = region.shape[0]
    tile_side = region.shape[1] - 2
    running = jnp.zeros((batch_count * tile_side * tile_side, kernel.shape[3]), jnp.float32)
    for step_y in range(3):
        for step_x in range(3):
            window = region[:, step_y:step_y + tile_side, step_x:step_x + tile_side, :]
            window = window.reshape(batch_count * tile_side * tile_side, region.shape[3])
            running = running + jnp.dot(window, kernel[step_y, step_x], preferred_element_type=jnp.float32)
    return (running + bias_vec).reshape(batch_count, tile_side, tile_side, kernel.shape[3])


def inside_cells(row_start, col_start, full_height, full_width, tile_side):
    row_ids = row_start[:, None] - 1 + jnp.arange(tile_side + 2, dtype=jnp.int32)[None, :]
    col_ids = col_start[:, None] - 1 + jnp.arange(tile_side + 2, dtype=jnp.int32)[None, :]
    row_ok = (row_ids >= 0) & (row_ids < full_height)
    col_ok = (col_ids >= 0) & (col_ids < full_width)
    return row_ok[:, :, None] & col_ok[:, None, :]


def first_conv(region, inside, kernel, bias_vec):
    hidden = conv_three(region, kernel, bias_vec)
    return jnp.where(inside[..., None], hidden, jnp.zeros((), hidden.dtype)).astype(jnp.bfloat16)


def second_conv(hidden, kernel, bias_vec):
    upsampled = jnp.repeat(jnp.repeat(hidden, 2, axis=1), 2, axis=2)
    cropped = upsampled[:, 1:-1, 1:-1, :]
    return conv_three(cropped, kernel, bias_vec).astype(jnp.bfloat16)


def reference(latent, gn_mean, gn_rstd, gn_gain, gn_shift, conv1_kernel, conv1_bias, conv2_kernel, conv2_bias, tile_dest):
    activated = norm_act(latent, gn_mean, gn_rstd, gn_gain, gn_shift)
    padded = jnp.pad(activated, ((2, 2), (2, 2), (0, 0)))

    def one_tile(tile_index):
        tile_row = (tile_index // TILES_C).astype(jnp.int32)
        tile_col = (tile_index % TILES_C).astype(jnp.int32)
        tile_code = tile_dest[tile_row, tile_col]

        def compute(unused):
            region = lax.dynamic_slice(padded, (tile_row * TS, tile_col * TS, jnp.int32(0)), (TS + 4, TS + 4, C))
            inside = inside_cells((tile_row * TS)[None], (tile_col * TS)[None], HEIGHT, WIDTH, TS)
            hidden = first_conv(region[None], inside, conv1_kernel, conv1_bias)
            return second_conv(hidden, conv2_kernel, conv2_bias)[0]

        def blank_tile(unused):
            return jnp.zeros((2 * TS, 2 * TS, C), jnp.bfloat16)

        return lax.cond(tile_code >= 0, compute, blank_tile, 0)

    tile_outputs = lax.map(one_tile, jnp.arange(TILES_R * TILES_C, dtype=jnp.int32))
    tile_outputs = tile_outputs.reshape(TILES_R, TILES_C, 2 * TS, 2 * TS, C).transpose(0, 2, 1, 3, 4)
    return tile_outputs.reshape(2 * HEIGHT, 2 * WIDTH, C)
```

```python
import functools

import jax
import jax.numpy as jnp
from jax import lax
from jax.experimental import pallas as pl
from jax.experimental.pallas import tpu as pltpu
from jax.sharding import PartitionSpec as P

TS = 3
TR = 4
TC = 4
ROWS = TR * TS
COLS = TC * TS
LANES = 128
PITCH = 16
F32 = jnp.float32
BF16 = jnp.bfloat16


def swaps(count, first):
    pairs = []
    for i in range(first, count - 1, 2):
        pairs += [(i, i + 1), (i + 1, i)]
    return pairs


def exchange(cells, axis, dim):
    count = lax.axis_size(axis)
    even = lax.axis_index(axis) % 2 == 0
    length = cells.shape[dim]
    head = lax.slice_in_dim(cells, 0, 2, axis=dim)
    tail = lax.slice_in_dim(cells, length - 2, length, axis=dim)
    from_even = lax.ppermute(jnp.where(even, tail, head), axis, swaps(count, 0))
    from_odd = lax.ppermute(jnp.where(even, head, tail), axis, swaps(count, 1))
    return from_even, from_odd


def sum_taps_kernel(w_ref, o_ref):
    chan = w_ref.shape[2]
    step, lanes = 16, 256

    def body(i, carry):
        rows = pl.ds(pl.multiple_of(i * step, step), step)
        for lane in range(0, w_ref.shape[3], lanes):
            cols = slice(lane, lane + lanes)
            k = [[w_ref[y, x, rows, cols].astype(F32) for x in range(3)] for y in range(3)]
            by_row = [
                [k[0][x] for x in range(3)],
                [k[1][x] + k[2][x] for x in range(3)],
                [k[0][x] + k[1][x] for x in range(3)],
                [k[2][x] for x in range(3)],
            ]
            for p in range(2):
                for a in range(2):
                    u = by_row[2 * p + a]
                    full = [u[0], u[1] + u[2], u[0] + u[1], u[2]]
                    for q in range(2):
                        for b in range(2):
                            at = pl.ds(pl.multiple_of((a * 2 + b) * chan + i * step, step), step)
                            o_ref[p, q, at, cols] = full[2 * q + b].astype(BF16)
        return carry

    lax.fori_loop(0, chan // step, body, 0)


def sum_taps(kernel):
    chan, outs = kernel.shape[2:]
    return pl.pallas_call(
        sum_taps_kernel,
        out_shape=jax.ShapeDtypeStruct((2, 2, 4 * chan, outs), BF16),
        in_specs=[pl.BlockSpec(memory_space=pltpu.VMEM)],
        out_specs=pl.BlockSpec(memory_space=pltpu.VMEM),
        compiler_params=pltpu.CompilerParams(vmem_limit_bytes=24 * 2**20),
        cost_estimate=pl.CostEstimate(flops=10_000_000, bytes_accessed=13_000_000, transcendentals=0),
        name="sum_taps",
    )(kernel)


def block_kernel(
    full_rows,
    full_cols,
    x_ref,
    row_even,
    row_odd,
    col_even,
    col_odd,
    mean_ref,
    rstd_ref,
    gain_ref,
    shift_ref,
    w1_ref,
    b1_ref,
    w2_ref,
    b2_ref,
    dest_ref,
    o_ref,
    act,
    taps,
    hid,
    packed,
    near,
    wide,
):
    chan = x_ref.shape[2]
    img = lax.axis_index("img")
    bal = lax.axis_index("bal")
    img_even = img % 2 == 0
    bal_even = bal % 2 == 0

    groups = mean_ref.shape[1]
    group_of = lax.broadcasted_iota(jnp.int32, (groups, chan), 1) // (chan // groups)
    spread = (lax.broadcasted_iota(jnp.int32, (groups, chan), 0) == group_of).astype(F32)
    exact = functools.partial(
        jnp.dot, precision=lax.Precision.HIGHEST, preferred_element_type=F32
    )
    mean = exact(jnp.broadcast_to(mean_ref[...], (8, groups)), spread)[0:1]
    rstd = exact(jnp.broadcast_to(rstd_ref[...], (8, groups)), spread)[0:1]
    gain = gain_ref[...]
    shift = shift_ref[...]

    def activate(cells):
        v = (cells.astype(F32) - mean) * rstd * gain + shift
        return v / (1.0 + jnp.exp(-v))

    def pick(even, even_ref, odd_ref, row):
        a, b = even_ref[row], odd_ref[row]
        return jnp.where(even, a, b), jnp.where(even, b, a)

    side = ROWS + 4
    for r in range(side):
        left, right = pick(bal_even, col_odd, col_even, r)
        if r < 2:
            mid = jnp.where(img_even, row_odd[r], row_even[r])
        elif r < ROWS + 2:
            mid = x_ref[r - 2]
        else:
            mid = jnp.where(img_even, row_even[r - 2 - ROWS], row_odd[r - 2 - ROWS])
        act[r * PITCH : r * PITCH + 2] = left.astype(F32)
        act[r * PITCH + 2 : r * PITCH + 2 + COLS] = mid.astype(F32)
        act[r * PITCH + 2 + COLS : (r + 1) * PITCH] = right.astype(F32)
    cell = lax.broadcasted_iota(jnp.int32, (PITCH, 1), 0)
    col = bal * COLS - 2 + cell
    col_ok = (col >= 0) & (col < full_cols)
    for r in range(side):
        row = img * ROWS - 2 + r
        ok = col_ok & ((row >= 0) & (row < full_rows))
        at = slice(r * PITCH, (r + 1) * PITCH)
        act[at] = jnp.where(ok, activate(act[at]), 0.0)
    total = side * PITCH
    act[total:] = jnp.zeros((act.shape[0] - total, chan), F32)
    for d in range(3):
        taps[:, d * chan : (d + 1) * chan] = act[d : d + total].astype(BF16)

    inner = (ROWS + 2) * PITCH
    h = b1_ref[...]
    for d in range(3):
        h = h + jnp.dot(
            taps[d * PITCH : d * PITCH + inner], w1_ref[d], preferred_element_type=F32
        )
    cell = lax.broadcasted_iota(jnp.int32, (inner, 1), 0)
    row = img * ROWS - 1 + cell // PITCH
    col = bal * COLS - 1 + cell % PITCH
    ok = (row >= 0) & (row < full_rows) & (col >= 0) & (col < full_cols)
    hid[0:inner] = jnp.where(ok, h, 0.0)

    for d in range(3):
        for r in range(ROWS + 2):
            packed[d, r * COLS : (r + 1) * COLS] = hid[r * PITCH + d : r * PITCH + d + COLS]
    count = ROWS * COLS
    for dy in range(3):
        for dx in range(3):
            at = (dy * 3 + dx) * chan
            near[:, at : at + chan] = packed[dx, dy * COLS : dy * COLS + count].astype(BF16)
    bias = b2_ref[...]
    for p in range(2):
        for q in range(2):
            z = bias
            for a in range(2):
                at = ((p + a) * 3 + q) * chan
                z = z + jnp.dot(
                    near[:, at : at + 2 * chan],
                    w2_ref[p, q, a * 2 * chan : (a + 1) * 2 * chan],
                    preferred_element_type=F32,
                )
            for r in range(ROWS):
                for k in range(wide.shape[0]):
                    lane = slice(k * LANES, (k + 1) * LANES)
                    wide[k, 2 * r + p, pl.ds(q, COLS, stride=2)] = z[r * COLS : (r + 1) * COLS, lane]
    cell = lax.broadcasted_iota(jnp.int32, (2 * COLS, 1), 0)
    for i in range(TR):
        live = jnp.zeros((2 * COLS, 1), jnp.int32)
        for j in range(TC):
            live = jnp.where(cell // (2 * TS) == j, (dest_ref[i, j] >= 0).astype(jnp.int32), live)
        for r in range(i * 2 * TS, (i + 1) * 2 * TS):
            for k in range(wide.shape[0]):
                lane = slice(k * LANES, (k + 1) * LANES)
                o_ref[r, :, lane] = jnp.where(live > 0, wide[k, r], 0.0).astype(BF16)


def run_block(full_rows, full_cols, *args):
    chan = args[0].shape[2]
    vmem = pl.BlockSpec(memory_space=pltpu.VMEM)
    smem = pl.BlockSpec(memory_space=pltpu.SMEM)
    side = ROWS + 4
    inner = (ROWS + 2) * PITCH
    count = ROWS * COLS
    return pl.pallas_call(
        functools.partial(block_kernel, full_rows, full_cols),
        out_shape=jax.ShapeDtypeStruct((2 * ROWS, 2 * COLS, chan), BF16),
        in_specs=[vmem] * 13 + [smem],
        out_specs=vmem,
        scratch_shapes=[
            pltpu.VMEM((side * PITCH + 8, chan), F32),
            pltpu.VMEM((side * PITCH, 3 * chan), BF16),
            pltpu.VMEM((inner + 8, chan), F32),
            pltpu.VMEM((3, (ROWS + 2) * COLS, chan), F32),
            pltpu.VMEM((count, 9 * chan), BF16),
            pltpu.VMEM((chan // LANES, 2 * ROWS, 2 * COLS, LANES), F32),
        ],
        compiler_params=pltpu.CompilerParams(vmem_limit_bytes=36 * 2**20),
        cost_estimate=pl.CostEstimate(
            flops=2_300_000_000, bytes_accessed=14_000_000, transcendentals=131_072
        ),
        name="decode_block",
    )(*args)


def shards(
    latent,
    gn_mean,
    gn_rstd,
    gn_gain,
    gn_shift,
    conv1_kernel,
    conv1_bias,
    conv2_kernel,
    conv2_bias,
    tile_dest,
):
    chan = latent.shape[2]
    full_rows = latent.shape[0] * lax.axis_size("img")
    full_cols = latent.shape[1] * lax.axis_size("bal")
    row_even, row_odd = exchange(latent, "img", 0)
    img_even = lax.axis_index("img") % 2 == 0
    above = jnp.where(img_even, row_odd, row_even)
    below = jnp.where(img_even, row_even, row_odd)
    tall = jnp.concatenate([above, latent, below], axis=0)
    col_even, col_odd = exchange(tall, "bal", 1)
    summed = sum_taps(conv2_kernel)
    return run_block(
        full_rows,
        full_cols,
        latent,
        row_even,
        row_odd,
        col_even,
        col_odd,
        gn_mean.reshape(1, -1),
        gn_rstd.reshape(1, -1),
        gn_gain.reshape(1, chan),
        gn_shift.reshape(1, chan),
        conv1_kernel.reshape(3, 3 * chan, -1),
        conv1_bias.reshape(1, -1),
        summed,
        conv2_bias.reshape(1, -1),
        tile_dest,
    )


def solution(mesh):
    placed = (P("img", "bal", None), P(), P(), P(), P(), P(), P(), P(), P(), P("img", "bal"))
    return jax.shard_map(
        shards, mesh=mesh, in_specs=placed, out_specs=P("img", "bal", None), check_vma=False
    )
```

```python
import functools

import jax
import jax.numpy as jnp
from jax import lax
from jax.experimental import pallas as pl
from jax.experimental.pallas import tpu as pltpu
from jax.sharding import PartitionSpec as P

TS = 3
TR = 4
TC = 4
ROWS = TR * TS
COLS = TC * TS
LANES = 128
PITCH = 16
F32 = jnp.float32
BF16 = jnp.bfloat16


def swaps(count, first):
    pairs = []
    for i in range(first, count - 1, 2):
        pairs += [(i, i + 1), (i + 1, i)]
    return pairs


def edges(cells, axis, dim):
    even = lax.axis_index(axis) % 2 == 0
    length = cells.shape[dim]
    head = lax.slice_in_dim(cells, 0, 2, axis=dim)
    tail = lax.slice_in_dim(cells, length - 2, length, axis=dim)
    return jnp.where(even, head, tail), jnp.where(even, tail, head)


def swap(edge_odd, edge_even, axis):
    count = lax.axis_size(axis)
    from_odd = lax.ppermute(edge_odd, axis, swaps(count, 1))
    from_even = lax.ppermute(edge_even, axis, swaps(count, 0))
    return from_odd, from_even


def sum_taps_kernel(w_hbm, o_ref, w_ref, sems):
    chan = w_ref.shape[2]
    step, lanes = 16, 256
    parts = sems.shape[0]
    depth = chan // parts
    copies = []
    for part in range(parts):
        at = pl.ds(part * depth, depth)
        copy = pltpu.make_async_copy(w_hbm.at[:, :, at], w_ref.at[:, :, at], sems.at[part])
        copy.start()
        copies.append(copy)

    def body(i, carry):
        rows = pl.ds(pl.multiple_of(i * step, step), step)
        for lane in range(0, w_ref.shape[3], lanes):
            cols = slice(lane, lane + lanes)
            k = [[w_ref[y, x, rows, cols].astype(F32) for x in range(3)] for y in range(3)]
            by_row = [
                [k[0][x] for x in range(3)],
                [k[1][x] + k[2][x] for x in range(3)],
                [k[0][x] + k[1][x] for x in range(3)],
                [k[2][x] for x in range(3)],
            ]
            for p in range(2):
                for a in range(2):
                    u = by_row[2 * p + a]
                    full = [u[0], u[1] + u[2], u[0] + u[1], u[2]]
                    for q in range(2):
                        for b in range(2):
                            at = pl.ds(pl.multiple_of((a * 2 + b) * chan + i * step, step), step)
                            o_ref[p, q, at, cols] = full[2 * q + b].astype(BF16)
        return carry

    for part in range(parts):
        copies[part].wait()
        lax.fori_loop(part * depth // step, (part + 1) * depth // step, body, 0)


def sum_taps(kernel):
    chan, outs = kernel.shape[2:]
    return pl.pallas_call(
        sum_taps_kernel,
        out_shape=jax.ShapeDtypeStruct((2, 2, 4 * chan, outs), BF16),
        in_specs=[pl.BlockSpec(memory_space=pltpu.HBM)],
        out_specs=pl.BlockSpec(memory_space=pltpu.VMEM),
        scratch_shapes=[pltpu.VMEM(kernel.shape, BF16), pltpu.SemaphoreType.DMA((4,))],
        compiler_params=pltpu.CompilerParams(vmem_limit_bytes=20 * 2**20),
        cost_estimate=pl.CostEstimate(flops=10_000_000, bytes_accessed=13_000_000, transcendentals=0),
        name="sum_taps",
    )(pltpu.with_memory_space_constraint(kernel, pltpu.HBM))


def block_kernel(
    full_rows,
    full_cols,
    x_ref,
    row_even,
    row_odd,
    col_odd,
    col_even,
    mean_ref,
    rstd_ref,
    gain_ref,
    shift_ref,
    w1_ref,
    b1_ref,
    w2_ref,
    b2_ref,
    dest_ref,
    o_ref,
    act,
    taps,
    hid,
    packed,
    near,
    wide,
):
    chan = x_ref.shape[2]
    img = lax.axis_index("img")
    bal = lax.axis_index("bal")
    img_even = img % 2 == 0
    bal_even = bal % 2 == 0

    groups = mean_ref.shape[1]
    group_of = lax.broadcasted_iota(jnp.int32, (groups, chan), 1) // (chan // groups)
    spread = (lax.broadcasted_iota(jnp.int32, (groups, chan), 0) == group_of).astype(F32)
    exact = functools.partial(
        jnp.dot, precision=lax.Precision.HIGHEST, preferred_element_type=F32
    )
    mean = exact(jnp.broadcast_to(mean_ref[...], (8, groups)), spread)[0:1]
    rstd = exact(jnp.broadcast_to(rstd_ref[...], (8, groups)), spread)[0:1]
    gain = gain_ref[...]
    shift = shift_ref[...]

    scale = 0.5 * rstd * gain
    offset = 0.5 * shift - mean * scale

    def activate(cells):
        v = cells * scale + offset
        return v * jnp.tanh(v) + v

    def pick(even, even_ref, odd_ref, row):
        a, b = even_ref[row], odd_ref[row]
        return jnp.where(even, a, b), jnp.where(even, b, a)

    side = ROWS + 4
    for r in range(side):
        left, right = pick(bal_even, col_odd, col_even, r)
        if r < 2:
            mid = jnp.where(img_even, row_odd[r], row_even[r])
        elif r < ROWS + 2:
            mid = x_ref[r - 2]
        else:
            mid = jnp.where(img_even, row_even[r - 2 - ROWS], row_odd[r - 2 - ROWS])
        act[r * PITCH : r * PITCH + 2] = left.astype(F32)
        act[r * PITCH + 2 : r * PITCH + 2 + COLS] = mid.astype(F32)
        act[r * PITCH + 2 + COLS : (r + 1) * PITCH] = right.astype(F32)
    cell = lax.broadcasted_iota(jnp.int32, (PITCH, 1), 0)
    col = bal * COLS - 2 + cell
    col_ok = (col >= 0) & (col < full_cols)
    for r in range(side):
        row = img * ROWS - 2 + r
        ok = col_ok & ((row >= 0) & (row < full_rows))
        at = slice(r * PITCH, (r + 1) * PITCH)
        act[at] = jnp.where(ok, activate(act[at]), 0.0)
    total = side * PITCH
    act[total:] = jnp.zeros((act.shape[0] - total, chan), F32)
    for d in range(3):
        taps[:, d * chan : (d + 1) * chan] = act[d : d + total].astype(BF16)

    inner = (ROWS + 2) * PITCH
    h = b1_ref[...]
    for d in range(3):
        h = h + jnp.dot(
            taps[d * PITCH : d * PITCH + inner], w1_ref[d], preferred_element_type=F32
        )
    cell = lax.broadcasted_iota(jnp.int32, (inner, 1), 0)
    row = img * ROWS - 1 + cell // PITCH
    col = bal * COLS - 1 + cell % PITCH
    ok = (row >= 0) & (row < full_rows) & (col >= 0) & (col < full_cols)
    hid[0:inner] = jnp.where(ok, h, 0.0)

    for d in range(3):
        for r in range(ROWS + 2):
            packed[d, r * COLS : (r + 1) * COLS] = hid[r * PITCH + d : r * PITCH + d + COLS]
    count = ROWS * COLS
    for dy in range(3):
        for dx in range(3):
            at = (dy * 3 + dx) * chan
            near[:, at : at + chan] = packed[dx, dy * COLS : dy * COLS + count].astype(BF16)
    bias = b2_ref[...]
    for p in range(2):
        for q in range(2):
            z = bias
            for a in range(2):
                at = ((p + a) * 3 + q) * chan
                z = z + jnp.dot(
                    near[:, at : at + 2 * chan],
                    w2_ref[p, q, a * 2 * chan : (a + 1) * 2 * chan],
                    preferred_element_type=F32,
                )
            for r in range(ROWS):
                for k in range(wide.shape[0]):
                    lane = slice(k * LANES, (k + 1) * LANES)
                    wide[k, 2 * r + p, pl.ds(q, COLS, stride=2)] = z[r * COLS : (r + 1) * COLS, lane]
    cell = lax.broadcasted_iota(jnp.int32, (2 * COLS, TC), 0)
    own = cell // (2 * TS) == lax.broadcasted_iota(jnp.int32, (2 * COLS, TC), 1)
    for i in range(TR):
        live = jnp.max(jnp.where(own, dest_ref[i : i + 1], -1), axis=1, keepdims=True)
        for r in range(i * 2 * TS, (i + 1) * 2 * TS):
            for k in range(wide.shape[0]):
                lane = slice(k * LANES, (k + 1) * LANES)
                o_ref[r, :, lane] = jnp.where(live >= 0, wide[k, r], 0.0).astype(BF16)


def run_block(full_rows, full_cols, *args):
    chan = args[0].shape[2]
    vmem = pl.BlockSpec(memory_space=pltpu.VMEM)
    side = ROWS + 4
    inner = (ROWS + 2) * PITCH
    count = ROWS * COLS
    return pl.pallas_call(
        functools.partial(block_kernel, full_rows, full_cols),
        out_shape=jax.ShapeDtypeStruct((2 * ROWS, 2 * COLS, chan), BF16),
        in_specs=[vmem] * 14,
        out_specs=vmem,
        scratch_shapes=[
            pltpu.VMEM((side * PITCH + 8, chan), F32),
            pltpu.VMEM((side * PITCH, 3 * chan), BF16),
            pltpu.VMEM((inner + 8, chan), F32),
            pltpu.VMEM((3, (ROWS + 2) * COLS, chan), F32),
            pltpu.VMEM((count, 9 * chan), BF16),
            pltpu.VMEM((chan // LANES, 2 * ROWS, 2 * COLS, LANES), F32),
        ],
        compiler_params=pltpu.CompilerParams(vmem_limit_bytes=36 * 2**20),
        cost_estimate=pl.CostEstimate(
            flops=2_300_000_000, bytes_accessed=14_000_000, transcendentals=131_072
        ),
        name="decode_block",
    )(*args)


def shards(
    latent,
    gn_mean,
    gn_rstd,
    gn_gain,
    gn_shift,
    conv1_kernel,
    conv1_bias,
    conv2_kernel,
    conv2_bias,
    tile_dest,
):
    chan = latent.shape[2]
    full_rows = latent.shape[0] * lax.axis_size("img")
    full_cols = latent.shape[1] * lax.axis_size("bal")
    row_odd, row_even = swap(*edges(latent, "img", 0), "img")
    col_own = lax.optimization_barrier(edges(latent, "bal", 1))
    img_even = lax.axis_index("img") % 2 == 0
    above = edges(jnp.where(img_even, row_odd, row_even), "bal", 1)
    below = edges(jnp.where(img_even, row_even, row_odd), "bal", 1)
    col_odd, col_even = swap(
        *(jnp.concatenate(part, axis=0) for part in zip(above, col_own, below)), "bal"
    )
    summed = sum_taps(conv2_kernel)
    return run_block(
        full_rows,
        full_cols,
        latent,
        row_even,
        row_odd,
        col_odd,
        col_even,
        gn_mean.reshape(1, -1),
        gn_rstd.reshape(1, -1),
        gn_gain.reshape(1, chan),
        gn_shift.reshape(1, chan),
        conv1_kernel.reshape(3, 3 * chan, -1),
        conv1_bias.reshape(1, -1),
        summed,
        conv2_bias.reshape(1, -1),
        tile_dest,
    )


def solution(mesh):
    placed = (P("img", "bal", None), P(), P(), P(), P(), P(), P(), P(), P(), P("img", "bal"))
    return jax.shard_map(
        shards, mesh=mesh, in_specs=placed, out_specs=P("img", "bal", None), check_vma=False
    )
```

```python
import functools

import jax
import jax.numpy as jnp
from jax import lax
from jax.experimental import pallas as pl
from jax.experimental.pallas import tpu as pltpu
from jax.sharding import PartitionSpec as P

TS = 3
TR = 4
TC = 4
ROWS = TR * TS
COLS = TC * TS
LANES = 128
SPLIT = 256
PITCH = 16
F32 = jnp.float32
BF16 = jnp.bfloat16


def swaps(count, first):
    pairs = []
    for i in range(first, count - 1, 2):
        pairs += [(i, i + 1), (i + 1, i)]
    return pairs


def edges(cells, axis, dim):
    even = lax.axis_index(axis) % 2 == 0
    length = cells.shape[dim]
    head = lax.slice_in_dim(cells, 0, 2, axis=dim)
    tail = lax.slice_in_dim(cells, length - 2, length, axis=dim)
    return jnp.where(even, head, tail), jnp.where(even, tail, head)


def swap(edge_odd, edge_even, axis):
    count = lax.axis_size(axis)
    from_odd = lax.ppermute(edge_odd, axis, swaps(count, 1))
    from_even = lax.ppermute(edge_even, axis, swaps(count, 0))
    return from_odd, from_even


def sum_taps_kernel(w_hbm, o_ref, w_ref, sems):
    chan = w_ref.shape[2]
    step, lanes = 16, 256
    parts = sems.shape[0]
    depth = chan // parts
    copies = []
    for part in range(parts):
        at = pl.ds(part * depth, depth)
        copy = pltpu.make_async_copy(w_hbm.at[:, :, at], w_ref.at[:, :, at], sems.at[part])
        copy.start()
        copies.append(copy)

    def body(i, carry):
        rows = pl.ds(pl.multiple_of(i * step, step), step)
        for lane in range(0, w_ref.shape[3], lanes):
            cols = slice(lane, lane + lanes)
            k = [[w_ref[y, x, rows, cols].astype(F32) for x in range(3)] for y in range(3)]
            for y, row in enumerate((k[0], [u + v + w for u, v, w in zip(*k)], k[2])):
                for x, tap in enumerate((row[0], row[0] + row[1] + row[2], row[2])):
                    o_ref[y, x, rows, cols] = tap.astype(BF16)
        return carry

    for part in range(parts):
        copies[part].wait()
        lax.fori_loop(part * depth // step, (part + 1) * depth // step, body, 0)


def sum_taps(kernel):
    return pl.pallas_call(
        sum_taps_kernel,
        out_shape=jax.ShapeDtypeStruct(kernel.shape, BF16),
        in_specs=[pl.BlockSpec(memory_space=pltpu.HBM)],
        out_specs=pl.BlockSpec(memory_space=pltpu.VMEM),
        scratch_shapes=[pltpu.VMEM(kernel.shape, BF16), pltpu.SemaphoreType.DMA((4,))],
        compiler_params=pltpu.CompilerParams(vmem_limit_bytes=20 * 2**20),
        cost_estimate=pl.CostEstimate(flops=10_000_000, bytes_accessed=13_000_000, transcendentals=0),
        name="sum_taps",
    )(pltpu.with_memory_space_constraint(kernel, pltpu.HBM))


def block_kernel(
    full_rows,
    full_cols,
    x_ref,
    row_even,
    row_odd,
    col_odd,
    col_even,
    mean_ref,
    rstd_ref,
    gain_ref,
    shift_ref,
    w1_ref,
    b1_ref,
    w2_ref,
    b2_ref,
    dest_ref,
    o_ref,
    act,
    taps,
    hid,
    packed,
    near,
    wide,
    done,
    sems,
):
    chan = x_ref.shape[2]
    img = lax.axis_index("img")
    bal = lax.axis_index("bal")
    img_even = img % 2 == 0
    bal_even = bal % 2 == 0

    groups = mean_ref.shape[1]
    group_of = lax.broadcasted_iota(jnp.int32, (groups, chan), 1) // (chan // groups)
    spread = (lax.broadcasted_iota(jnp.int32, (groups, chan), 0) == group_of).astype(F32)
    exact = functools.partial(
        jnp.dot, precision=lax.Precision.HIGHEST, preferred_element_type=F32
    )
    mean = exact(jnp.broadcast_to(mean_ref[...], (8, groups)), spread)[0:1]
    rstd = exact(jnp.broadcast_to(rstd_ref[...], (8, groups)), spread)[0:1]
    gain = gain_ref[...]
    shift = shift_ref[...]

    scale = 0.5 * rstd * gain
    offset = 0.5 * shift - mean * scale

    def activate(cells):
        v = cells * scale + offset
        return v * jnp.tanh(v) + v

    def pick(even, even_ref, odd_ref, row):
        a, b = even_ref[row], odd_ref[row]
        return jnp.where(even, a, b), jnp.where(even, b, a)

    side = ROWS + 4
    for r in range(side):
        left, right = pick(bal_even, col_odd, col_even, r)
        if r < 2:
            mid = jnp.where(img_even, row_odd[r], row_even[r])
        elif r < ROWS + 2:
            mid = x_ref[r - 2]
        else:
            mid = jnp.where(img_even, row_even[r - 2 - ROWS], row_odd[r - 2 - ROWS])
        act[r * PITCH : r * PITCH + 2] = left.astype(F32)
        act[r * PITCH + 2 : r * PITCH + 2 + COLS] = mid.astype(F32)
        act[r * PITCH + 2 + COLS : (r + 1) * PITCH] = right.astype(F32)
    cell = lax.broadcasted_iota(jnp.int32, (PITCH, 1), 0)
    col = bal * COLS - 2 + cell
    col_ok = (col >= 0) & (col < full_cols)
    for r in range(side):
        row = img * ROWS - 2 + r
        ok = col_ok & ((row >= 0) & (row < full_rows))
        at = slice(r * PITCH, (r + 1) * PITCH)
        act[at] = jnp.where(ok, activate(act[at]), 0.0)
    total = side * PITCH
    act[total:] = jnp.zeros((act.shape[0] - total, chan), F32)
    for d in range(3):
        taps[:, d * chan : (d + 1) * chan] = act[d : d + total].astype(BF16)

    inner = (ROWS + 2) * PITCH
    cell = lax.broadcasted_iota(jnp.int32, (inner, 1), 0)
    row = img * ROWS - 1 + cell // PITCH
    col = bal * COLS - 1 + cell % PITCH
    ok = (row >= 0) & (row < full_rows) & (col >= 0) & (col < full_cols)
    count = ROWS * COLS
    parts = [slice(n, n + SPLIT) for n in range(0, chan, SPLIT)]

    for part in parts:
        h = b1_ref[:, part]
        for d in range(3):
            h = h + jnp.dot(
                taps[d * PITCH : d * PITCH + inner], w1_ref[d, :, part], preferred_element_type=F32
            )
        hid[0:inner, part] = jnp.where(ok, h, 0.0).astype(BF16).astype(F32)
        for d in range(3):
            for r in range(ROWS + 2):
                at = r * PITCH + d
                packed[d, r * COLS : (r + 1) * COLS, part] = hid[at : at + COLS, part]
        packed[0, :, part] = packed[0, :, part] - packed[1, :, part]
        packed[2, :, part] = packed[2, :, part] - packed[1, :, part]
        for dx in range(3):
            here = packed[dx, COLS : COLS + count, part]
            for dy in range(3):
                at = (dy * 3 + dx) * chan + part.start
                cells = here
                if dy != 1:
                    cells = packed[dx, dy * COLS : dy * COLS + count, part] - here
                near[:, at : at + SPLIT] = cells.astype(BF16)

    cell = lax.broadcasted_iota(jnp.int32, (2 * COLS, TC), 0)
    own = cell // (2 * TS) == lax.broadcasted_iota(jnp.int32, (2 * COLS, TC), 1)
    live = [
        jnp.max(jnp.where(own, dest_ref[i : i + 1], -1), axis=1, keepdims=True) >= 0
        for i in range(TR)
    ]
    copies = []
    for n, part in enumerate(parts):

        def term(dy, dx):
            at = (dy * 3 + dx) * chan
            return jnp.dot(
                near[:, at : at + chan], w2_ref[dy, dx, :, part], preferred_element_type=F32
            )

        base = term(1, 1) + b2_ref[:, part]
        by_row = [base + term(0, 1), base + term(2, 1)]
        lanes = range(part.start // LANES, part.stop // LANES)
        for q in range(2):
            by_col = term(1, 2 * q)
            for p in range(2):
                z = by_row[p] + by_col + term(2 * p, 2 * q)
                for r in range(ROWS):
                    for k in lanes:
                        at = k * LANES - part.start
                        wide[k, 2 * r + p, pl.ds(q, COLS, stride=2)] = z[
                            r * COLS : (r + 1) * COLS, at : at + LANES
                        ]
        for r in range(2 * ROWS):
            for k in lanes:
                lane = slice(k * LANES, (k + 1) * LANES)
                kept = jnp.where(live[r // (2 * TS)], wide[k, r], 0.0)
                done[r, :, lane] = kept.astype(BF16)
        copy = pltpu.make_async_copy(done.at[:, :, part], o_ref.at[:, :, part], sems.at[n])
        copy.start()
        copies.append(copy)
    for copy in copies:
        copy.wait()


def run_block(full_rows, full_cols, *args):
    chan = args[0].shape[2]
    vmem = pl.BlockSpec(memory_space=pltpu.VMEM)
    side = ROWS + 4
    inner = (ROWS + 2) * PITCH
    count = ROWS * COLS
    return pl.pallas_call(
        functools.partial(block_kernel, full_rows, full_cols),
        out_shape=jax.ShapeDtypeStruct((2 * ROWS, 2 * COLS, chan), BF16),
        in_specs=[vmem] * 14,
        out_specs=pl.BlockSpec(memory_space=pltpu.HBM),
        scratch_shapes=[
            pltpu.VMEM((side * PITCH + 8, chan), F32),
            pltpu.VMEM((side * PITCH, 3 * chan), BF16),
            pltpu.VMEM((inner + 8, chan), F32),
            pltpu.VMEM((3, (ROWS + 2) * COLS, chan), F32),
            pltpu.VMEM((count, 9 * chan), BF16),
            pltpu.VMEM((chan // LANES, 2 * ROWS, 2 * COLS, LANES), F32),
            pltpu.VMEM((2 * ROWS, 2 * COLS, chan), BF16),
            pltpu.SemaphoreType.DMA((chan // SPLIT,)),
        ],
        compiler_params=pltpu.CompilerParams(vmem_limit_bytes=36 * 2**20),
        cost_estimate=pl.CostEstimate(
            flops=2_300_000_000, bytes_accessed=14_000_000, transcendentals=131_072
        ),
        name="decode_block",
    )(*args)


def shards(
    latent,
    gn_mean,
    gn_rstd,
    gn_gain,
    gn_shift,
    conv1_kernel,
    conv1_bias,
    conv2_kernel,
    conv2_bias,
    tile_dest,
):
    chan = latent.shape[2]
    full_rows = latent.shape[0] * lax.axis_size("img")
    full_cols = latent.shape[1] * lax.axis_size("bal")
    row_odd, row_even = swap(*edges(latent, "img", 0), "img")
    col_own = lax.optimization_barrier(edges(latent, "bal", 1))
    img_even = lax.axis_index("img") % 2 == 0
    above = edges(jnp.where(img_even, row_odd, row_even), "bal", 1)
    below = edges(jnp.where(img_even, row_even, row_odd), "bal", 1)
    col_odd, col_even = swap(
        *(jnp.concatenate(part, axis=0) for part in zip(above, col_own, below)), "bal"
    )
    summed = sum_taps(conv2_kernel)
    return run_block(
        full_rows,
        full_cols,
        latent,
        row_even,
        row_odd,
        col_odd,
        col_even,
        gn_mean.reshape(1, -1),
        gn_rstd.reshape(1, -1),
        gn_gain.reshape(1, chan),
        gn_shift.reshape(1, chan),
        conv1_kernel.reshape(3, 3 * chan, -1),
        conv1_bias.reshape(1, -1),
        summed,
        conv2_bias.reshape(1, -1),
        tile_dest,
    )


def solution(mesh):
    placed = (P("img", "bal", None), P(), P(), P(), P(), P(), P(), P(), P(), P("img", "bal"))
    return jax.shard_map(
        shards, mesh=mesh, in_specs=placed, out_specs=P("img", "bal", None), check_vma=False
    )
```

```python
import functools

import jax
import jax.numpy as jnp
from jax import lax
from jax.experimental import pallas as pl
from jax.experimental.pallas import tpu as pltpu
from jax.sharding import PartitionSpec as P

TS = 3
TR = 4
TC = 4
ROWS = TR * TS
COLS = TC * TS
LANES = 128
STEP = 16
SPLIT = 256
PITCH = 16
F32 = jnp.float32
BF16 = jnp.bfloat16


def swaps(count, first):
    pairs = []
    for i in range(first, count - 1, 2):
        pairs += [(i, i + 1), (i + 1, i)]
    return pairs


def pair_groups(rows, cols):
    img = [[i * cols + j, (i + 1) * cols + j] for i in range(0, rows, 2) for j in range(cols)]
    bal = [[i * cols + j, i * cols + j + 1] for i in range(rows) for j in range(0, cols, 2)]
    return img, bal


def rows_kernel(x_hbm, w1_hbm, w2_hbm, core_ref, z_ref, sems):
    img_even = lax.axis_index("img") % 2 == 0
    last = x_hbm.shape[0] - 2
    core_at = jnp.where(img_even, last, 0)
    copies = [
        pltpu.make_async_copy(x_hbm.at[pl.ds(at, 2)], ref, sems.at[n])
        for n, (at, ref) in enumerate(((last - core_at, z_ref), (core_at, core_ref)))
    ]
    for copy in copies:
        copy.start()
    for copy in copies:
        copy.wait()


def row_edges(x, w1, w2):
    vmem = pl.BlockSpec(memory_space=pltpu.VMEM)
    edge = jax.ShapeDtypeStruct((2,) + x.shape[1:], BF16)
    return pl.pallas_call(
        rows_kernel,
        out_shape=(edge, edge),
        in_specs=[pl.BlockSpec(memory_space=pltpu.HBM)] * 3,
        out_specs=(vmem, vmem),
        scratch_shapes=[pltpu.SemaphoreType.DMA((2,))],
        compiler_params=pltpu.CompilerParams(vmem_limit_bytes=4 * 2**20),
        cost_estimate=pl.CostEstimate(flops=0, bytes_accessed=30_000_000, transcendentals=0),
        name="row_edges",
    )(*(pltpu.with_memory_space_constraint(a, pltpu.HBM) for a in (x, w1, w2)))


def columns_kernel(x_ref, row_z, row_core, w1_hbm, w2_hbm, odd_ref, even_ref):
    img_even = lax.axis_index("img") % 2 == 0
    bal_even = lax.axis_index("bal") % 2 == 0
    last = x_ref.shape[1]

    def put(row, cells):
        head, tail = cells[0:2], cells[last - 2 : last]
        odd_ref[row] = jnp.where(bal_even, head, tail)
        even_ref[row] = jnp.where(bal_even, tail, head)

    for r in range(2):
        put(r, jnp.where(img_even, row_z[r], row_core[0, r]))
        put(r + 2 + ROWS, jnp.where(img_even, row_core[1, r], row_z[r]))
    for r in range(ROWS):
        put(r + 2, x_ref[r])


def column_edges(x, row_z, row_core, w1, w2):
    vmem = pl.BlockSpec(memory_space=pltpu.VMEM)
    edge = jax.ShapeDtypeStruct((ROWS + 4, 2, x.shape[2]), BF16)
    return pl.pallas_call(
        columns_kernel,
        out_shape=(edge, edge),
        in_specs=[vmem] * 3 + [pl.BlockSpec(memory_space=pltpu.HBM)] * 2,
        out_specs=(vmem, vmem),
        compiler_params=pltpu.CompilerParams(vmem_limit_bytes=4 * 2**20),
        cost_estimate=pl.CostEstimate(flops=0, bytes_accessed=30_000_000, transcendentals=0),
        name="column_edges",
    )(x, row_z, row_core, *(pltpu.with_memory_space_constraint(a, pltpu.HBM) for a in (w1, w2)))


def block_kernel(
    full_rows,
    full_cols,
    x_ref,
    row_z,
    row_core,
    col_odd,
    col_even,
    mean_ref,
    rstd_ref,
    gain_ref,
    shift_ref,
    w1_ref,
    b1_ref,
    w2_ref,
    b2_ref,
    dest_ref,
    o_ref,
    act,
    taps,
    hid,
    packed,
    near,
    wide,
    done,
    sums,
    sems,
):
    chan = x_ref.shape[2]
    img = lax.axis_index("img")
    bal = lax.axis_index("bal")
    img_even = img % 2 == 0
    bal_even = bal % 2 == 0

    groups = mean_ref.shape[1]
    group_of = lax.broadcasted_iota(jnp.int32, (groups, chan), 1) // (chan // groups)
    spread = (lax.broadcasted_iota(jnp.int32, (groups, chan), 0) == group_of).astype(F32)
    exact = functools.partial(
        jnp.dot, precision=lax.Precision.HIGHEST, preferred_element_type=F32
    )
    mean = exact(jnp.broadcast_to(mean_ref[...], (8, groups)), spread)[0:1]
    rstd = exact(jnp.broadcast_to(rstd_ref[...], (8, groups)), spread)[0:1]
    gain = gain_ref[...]
    shift = shift_ref[...]

    scale = 0.5 * rstd * gain
    offset = 0.5 * shift - mean * scale

    def activate(cells):
        v = cells * scale + offset
        return v * jnp.tanh(v) + v

    side = ROWS + 4
    lines = [x_ref[r] for r in range(ROWS)]
    lines = [jnp.where(img_even, row_z[r], row_core[0, r]) for r in range(2)] + lines
    lines += [jnp.where(img_even, row_core[1, r], row_z[r]) for r in range(2)]
    for r, line in enumerate(lines):
        left = jnp.where(bal_even, col_odd[r], col_even[0, r])
        right = jnp.where(bal_even, col_even[1, r], col_odd[r])
        at = r * PITCH
        act[at : at + 2] = left.astype(F32)
        act[at + 2 : at + 2 + COLS] = line.astype(F32)
        act[at + 2 + COLS : at + PITCH] = right.astype(F32)
    cell = lax.broadcasted_iota(jnp.int32, (PITCH, 1), 0)
    col = bal * COLS - 2 + cell
    col_ok = (col >= 0) & (col < full_cols)
    for r in range(side):
        row = img * ROWS - 2 + r
        ok = col_ok & ((row >= 0) & (row < full_rows))
        at = slice(r * PITCH, (r + 1) * PITCH)
        act[at] = jnp.where(ok, activate(act[at]), 0.0)
    total = side * PITCH
    act[total:] = jnp.zeros((act.shape[0] - total, chan), F32)
    for d in range(3):
        taps[:, d * chan : (d + 1) * chan] = act[d : d + total].astype(BF16)

    inner = (ROWS + 2) * PITCH
    cell = lax.broadcasted_iota(jnp.int32, (inner, 1), 0)
    row = img * ROWS - 1 + cell // PITCH
    col = bal * COLS - 1 + cell % PITCH
    ok = (row >= 0) & (row < full_rows) & (col >= 0) & (col < full_cols)
    count = ROWS * COLS
    parts = [slice(n, n + SPLIT) for n in range(0, chan, SPLIT)]

    summed = [(0, 1), (1, 0), (1, 1), (1, 2), (2, 1)]

    def sum_taps(first, stop):
        for at in range(first, stop, STEP):
            rows = slice(at, at + STEP)
            for lane in range(0, chan, SPLIT):
                cols = slice(lane, lane + SPLIT)
                k = [[w2_ref[y, x, rows, cols].astype(F32) for x in range(3)] for y in range(3)]
                down = [u + v + w for u, v, w in zip(*k)]
                full = (sum(k[0]), down[0], sum(down), down[2], sum(k[2]))
                for n, tap in enumerate(full):
                    sums[n, rows, cols] = tap.astype(BF16)

    turns = 3 * len(parts)
    marks = [chan // STEP * turn // turns * STEP for turn in range(turns + 1)]
    for n, part in enumerate(parts):
        h = b1_ref[:, part]
        for d in range(3):
            h = h + jnp.dot(
                taps[d * PITCH : d * PITCH + inner], w1_ref[d, :, part], preferred_element_type=F32
            )
            sum_taps(marks[3 * n + d], marks[3 * n + d + 1])
        hid[0:inner, part] = jnp.where(ok, h, 0.0).astype(BF16).astype(F32)
        for d in range(3):
            for r in range(ROWS + 2):
                at = r * PITCH + d
                packed[d, r * COLS : (r + 1) * COLS, part] = hid[at : at + COLS, part]
        packed[0, :, part] = packed[0, :, part] - packed[1, :, part]
        packed[2, :, part] = packed[2, :, part] - packed[1, :, part]
        for dx in range(3):
            here = packed[dx, COLS : COLS + count, part]
            for dy in range(3):
                at = (dy * 3 + dx) * chan + part.start
                cells = here
                if dy != 1:
                    cells = packed[dx, dy * COLS : dy * COLS + count, part] - here
                near[:, at : at + SPLIT] = cells.astype(BF16)

    cell = lax.broadcasted_iota(jnp.int32, (2 * COLS, TC), 0)
    own = cell // (2 * TS) == lax.broadcasted_iota(jnp.int32, (2 * COLS, TC), 1)
    live = [
        jnp.max(jnp.where(own, dest_ref[i : i + 1], -1), axis=1, keepdims=True) >= 0
        for i in range(TR)
    ]
    copies = []
    for n, part in enumerate(parts):

        def term(dy, dx):
            at = (dy * 3 + dx) * chan
            if (dy, dx) in summed:
                w = sums[summed.index((dy, dx)), :, part]
            else:
                w = w2_ref[dy, dx, :, part]
            return jnp.dot(near[:, at : at + chan], w, preferred_element_type=F32)

        base = term(1, 1) + b2_ref[:, part]
        by_row = [base + term(0, 1), base + term(2, 1)]
        lanes = range(part.start // LANES, part.stop // LANES)
        for q in range(2):
            by_col = term(1, 2 * q)
            for p in range(2):
                z = by_row[p] + by_col + term(2 * p, 2 * q)
                for r in range(ROWS):
                    for k in lanes:
                        at = k * LANES - part.start
                        wide[k, 2 * r + p, pl.ds(q, COLS, stride=2)] = z[
                            r * COLS : (r + 1) * COLS, at : at + LANES
                        ]
        for r in range(2 * ROWS):
            for k in lanes:
                lane = slice(k * LANES, (k + 1) * LANES)
                kept = jnp.where(live[r // (2 * TS)], wide[k, r], 0.0)
                done[r, :, lane] = kept.astype(BF16)
        copy = pltpu.make_async_copy(done.at[:, :, part], o_ref.at[:, :, part], sems.at[n])
        copy.start()
        copies.append(copy)
    for copy in copies:
        copy.wait()


def run_block(full_rows, full_cols, *args):
    chan = args[0].shape[2]
    vmem = pl.BlockSpec(memory_space=pltpu.VMEM)
    side = ROWS + 4
    inner = (ROWS + 2) * PITCH
    count = ROWS * COLS
    return pl.pallas_call(
        functools.partial(block_kernel, full_rows, full_cols),
        out_shape=jax.ShapeDtypeStruct((2 * ROWS, 2 * COLS, chan), BF16),
        in_specs=[vmem] * 14,
        out_specs=pl.BlockSpec(memory_space=pltpu.HBM),
        scratch_shapes=[
            pltpu.VMEM((side * PITCH + 8, chan), F32),
            pltpu.VMEM((side * PITCH, 3 * chan), BF16),
            pltpu.VMEM((inner + 8, chan), F32),
            pltpu.VMEM((3, (ROWS + 2) * COLS, chan), F32),
            pltpu.VMEM((count, 9 * chan), BF16),
            pltpu.VMEM((chan // LANES, 2 * ROWS, 2 * COLS, LANES), F32),
            pltpu.VMEM((2 * ROWS, 2 * COLS, chan), BF16),
            pltpu.VMEM((5, chan, chan), BF16),
            pltpu.SemaphoreType.DMA((chan // SPLIT,)),
        ],
        compiler_params=pltpu.CompilerParams(vmem_limit_bytes=36 * 2**20),
        cost_estimate=pl.CostEstimate(
            flops=2_300_000_000, bytes_accessed=14_000_000, transcendentals=131_072
        ),
        name="decode_block",
    )(*args)


def shards(
    latent,
    gn_mean,
    gn_rstd,
    gn_gain,
    gn_shift,
    conv1_kernel,
    conv1_bias,
    conv2_kernel,
    conv2_bias,
    tile_dest,
):
    chan = latent.shape[2]
    full_rows = latent.shape[0] * lax.axis_size("img")
    full_cols = latent.shape[1] * lax.axis_size("bal")
    mesh_axes = ("img", "bal")
    core_pairs, even_pairs = pair_groups(lax.axis_size("img"), lax.axis_size("bal"))
    edge_core, edge_z = row_edges(latent, conv1_kernel, conv2_kernel)
    row_z = lax.ppermute(edge_z, "img", swaps(lax.axis_size("img"), 1))
    row_core = lax.all_gather(edge_core, mesh_axes, axis_index_groups=core_pairs)
    edge_odd, edge_even = column_edges(latent, row_z, row_core, conv1_kernel, conv2_kernel)
    col_odd = lax.ppermute(edge_odd, "bal", swaps(lax.axis_size("bal"), 1))
    col_even = lax.all_gather(edge_even, mesh_axes, axis_index_groups=even_pairs)
    return run_block(
        full_rows,
        full_cols,
        latent,
        row_z,
        row_core,
        col_odd,
        col_even,
        gn_mean.reshape(1, -1),
        gn_rstd.reshape(1, -1),
        gn_gain.reshape(1, chan),
        gn_shift.reshape(1, chan),
        conv1_kernel.reshape(3, 3 * chan, -1),
        conv1_bias.reshape(1, -1),
        conv2_kernel,
        conv2_bias.reshape(1, -1),
        tile_dest,
    )


def solution(mesh):
    placed = (P("img", "bal", None), P(), P(), P(), P(), P(), P(), P(), P(), P("img", "bal"))
    return jax.shard_map(
        shards, mesh=mesh, in_specs=placed, out_specs=P("img", "bal", None), check_vma=False
    )
```

```python
import functools

import jax
import jax.numpy as jnp
from jax import lax
from jax.experimental import pallas as pl
from jax.experimental.pallas import tpu as pltpu
from jax.sharding import PartitionSpec as P

TS = 3
TR = 4
TC = 4
ROWS = TR * TS
COLS = TC * TS
LANES = 128
SPLIT = 256
PITCH = 16
F32 = jnp.float32
BF16 = jnp.bfloat16


def swaps(count, first):
    pairs = []
    for i in range(first, count - 1, 2):
        pairs += [(i, i + 1), (i + 1, i)]
    return pairs


def pair_groups(rows, cols):
    img = [[i * cols + j, (i + 1) * cols + j] for i in range(0, rows, 2) for j in range(cols)]
    bal = [[i * cols + j, i * cols + j + 1] for i in range(rows) for j in range(0, cols, 2)]
    return img, bal


def rows_kernel(x_hbm, w1_hbm, w2_hbm, core_ref, z_ref, sems):
    img_even = lax.axis_index("img") % 2 == 0
    last = x_hbm.shape[0] - 2
    core_at = jnp.where(img_even, last, 0)
    copies = [
        pltpu.make_async_copy(x_hbm.at[pl.ds(at, 2)], ref, sems.at[n])
        for n, (at, ref) in enumerate(((last - core_at, z_ref), (core_at, core_ref)))
    ]
    for copy in copies:
        copy.start()
    for copy in copies:
        copy.wait()


def row_edges(x, w1, w2):
    vmem = pl.BlockSpec(memory_space=pltpu.VMEM)
    edge = jax.ShapeDtypeStruct((2,) + x.shape[1:], BF16)
    return pl.pallas_call(
        rows_kernel,
        out_shape=(edge, edge),
        in_specs=[pl.BlockSpec(memory_space=pltpu.HBM)] * 3,
        out_specs=(vmem, vmem),
        scratch_shapes=[pltpu.SemaphoreType.DMA((2,))],
        compiler_params=pltpu.CompilerParams(vmem_limit_bytes=4 * 2**20),
        cost_estimate=pl.CostEstimate(flops=0, bytes_accessed=30_000_000, transcendentals=0),
        name="row_edges",
    )(*(pltpu.with_memory_space_constraint(a, pltpu.HBM) for a in (x, w1, w2)))


def columns_kernel(x_ref, row_z, row_core, w1_hbm, w2_hbm, odd_ref, even_ref):
    img_even = lax.axis_index("img") % 2 == 0
    bal_even = lax.axis_index("bal") % 2 == 0
    last = x_ref.shape[1]

    def put(row, cells):
        head, tail = cells[0:2], cells[last - 2 : last]
        odd_ref[row] = jnp.where(bal_even, head, tail)
        even_ref[row] = jnp.where(bal_even, tail, head)

    for r in range(2):
        put(r, jnp.where(img_even, row_z[r], row_core[0, r]))
        put(r + 2 + ROWS, jnp.where(img_even, row_core[1, r], row_z[r]))
    for r in range(ROWS):
        put(r + 2, x_ref[r])


def column_edges(x, row_z, row_core, w1, w2):
    vmem = pl.BlockSpec(memory_space=pltpu.VMEM)
    edge = jax.ShapeDtypeStruct((ROWS + 4, 2, x.shape[2]), BF16)
    return pl.pallas_call(
        columns_kernel,
        out_shape=(edge, edge),
        in_specs=[vmem] * 3 + [pl.BlockSpec(memory_space=pltpu.HBM)] * 2,
        out_specs=(vmem, vmem),
        compiler_params=pltpu.CompilerParams(vmem_limit_bytes=4 * 2**20),
        cost_estimate=pl.CostEstimate(flops=0, bytes_accessed=30_000_000, transcendentals=0),
        name="column_edges",
    )(x, row_z, row_core, *(pltpu.with_memory_space_constraint(a, pltpu.HBM) for a in (w1, w2)))


def block_kernel(
    full_rows,
    full_cols,
    x_ref,
    row_z,
    row_core,
    col_odd,
    col_even,
    mean_ref,
    rstd_ref,
    gain_ref,
    shift_ref,
    w1_ref,
    b1_ref,
    w2_ref,
    b2_ref,
    dest_ref,
    o_ref,
    act,
    taps,
    hid,
    near,
    wide,
    done,
    sems,
):
    chan = x_ref.shape[2]
    img = lax.axis_index("img")
    bal = lax.axis_index("bal")
    img_even = img % 2 == 0
    bal_even = bal % 2 == 0

    groups = mean_ref.shape[1]
    group_of = lax.broadcasted_iota(jnp.int32, (groups, chan), 1) // (chan // groups)
    spread = (lax.broadcasted_iota(jnp.int32, (groups, chan), 0) == group_of).astype(F32)
    exact = functools.partial(
        jnp.dot, precision=lax.Precision.HIGHEST, preferred_element_type=F32
    )
    mean = exact(jnp.broadcast_to(mean_ref[...], (8, groups)), spread)[0:1]
    rstd = exact(jnp.broadcast_to(rstd_ref[...], (8, groups)), spread)[0:1]
    gain = gain_ref[...]
    shift = shift_ref[...]

    scale = 0.5 * rstd * gain
    offset = 0.5 * shift - mean * scale

    def activate(cells):
        v = cells * scale + offset
        return v * jnp.tanh(v) + v

    side = ROWS + 4
    lines = [x_ref[r] for r in range(ROWS)]
    lines = [jnp.where(img_even, row_z[r], row_core[0, r]) for r in range(2)] + lines
    lines += [jnp.where(img_even, row_core[1, r], row_z[r]) for r in range(2)]
    for r, line in enumerate(lines):
        left = jnp.where(bal_even, col_odd[r], col_even[0, r])
        right = jnp.where(bal_even, col_even[1, r], col_odd[r])
        at = r * PITCH
        act[at : at + 2] = left.astype(F32)
        act[at + 2 : at + 2 + COLS] = line.astype(F32)
        act[at + 2 + COLS : at + PITCH] = right.astype(F32)
    cell = lax.broadcasted_iota(jnp.int32, (PITCH, 1), 0)
    col = bal * COLS - 2 + cell
    col_ok = (col >= 0) & (col < full_cols)
    for r in range(side):
        row = img * ROWS - 2 + r
        ok = col_ok & ((row >= 0) & (row < full_rows))
        at = slice(r * PITCH, (r + 1) * PITCH)
        act[at] = jnp.where(ok, activate(act[at]), 0.0)
    total = side * PITCH
    act[total:] = jnp.zeros((act.shape[0] - total, chan), F32)
    for d in range(3):
        taps[:, d * chan : (d + 1) * chan] = act[d : d + total].astype(BF16)

    inner = (ROWS + 2) * PITCH
    cell = lax.broadcasted_iota(jnp.int32, (inner, 1), 0)
    row = img * ROWS - 1 + cell // PITCH
    col = bal * COLS - 1 + cell % PITCH
    ok = (row >= 0) & (row < full_rows) & (col >= 0) & (col < full_cols)
    parts = [slice(n, n + SPLIT) for n in range(0, chan, SPLIT)]

    for part in parts:
        h = b1_ref[:, part]
        for e in range(3):
            lane = slice(e * chan, (e + 1) * chan)
            for d in range(3):
                h = h + jnp.dot(
                    taps[d * PITCH : d * PITCH + inner, lane],
                    w1_ref[d, lane, part],
                    preferred_element_type=F32,
                )
        hid[:, part] = jnp.where(ok, h, 0.0).astype(BF16)

    cell = lax.broadcasted_iota(jnp.int32, (2 * COLS, TC), 0)
    own = cell // (2 * TS) == lax.broadcasted_iota(jnp.int32, (2 * COLS, TC), 1)
    live = [
        jnp.max(jnp.where(own, dest_ref[i : i + 1], -1), axis=1, keepdims=True) >= 0
        for i in range(TR)
    ]
    copies = []
    for n, part in enumerate(parts):

        lanes = range(part.start // LANES, part.stop // LANES)
        span = ROWS * PITCH
        by_row = [[], []]
        for dx in range(3):
            first, mid, last = [
                jnp.dot(hid[...], w2_ref[dy, dx, :, part], preferred_element_type=F32)
                for dy in range(3)
            ]
            here = slice(PITCH, PITCH + span)
            by_row[0].append(first[:span] + (mid[here] + last[here]))
            by_row[1].append((first[here] + mid[here]) + last[2 * PITCH :])
        bias = b2_ref[:, part]
        for p in range(2):
            left, mid, right = by_row[p]
            mid = mid + bias
            near[0, :span] = mid + right
            near[1, :span] = mid + left
            near[2, :span] = right
            for r in range(ROWS):
                at = r * PITCH
                zs = (
                    left[at : at + COLS] + near[0, at + 1 : at + 1 + COLS],
                    near[1, at + 1 : at + 1 + COLS] + near[2, at + 2 : at + 2 + COLS],
                )
                for q, z in enumerate(zs):
                    for n_lane, k in enumerate(lanes):
                        wide[k, 2 * r + p, pl.ds(q, COLS, stride=2)] = z[
                            :, n_lane * LANES : (n_lane + 1) * LANES
                        ]
        for r in range(2 * ROWS):
            for k in lanes:
                lane = slice(k * LANES, (k + 1) * LANES)
                kept = jnp.where(live[r // (2 * TS)], wide[k, r], 0.0)
                done[r, :, lane] = kept.astype(BF16)
        copy = pltpu.make_async_copy(done.at[:, :, part], o_ref.at[:, :, part], sems.at[n])
        copy.start()
        copies.append(copy)
    for copy in copies:
        copy.wait()


def run_block(full_rows, full_cols, *args):
    chan = args[0].shape[2]
    vmem = pl.BlockSpec(memory_space=pltpu.VMEM)
    side = ROWS + 4
    inner = (ROWS + 2) * PITCH
    return pl.pallas_call(
        functools.partial(block_kernel, full_rows, full_cols),
        out_shape=jax.ShapeDtypeStruct((2 * ROWS, 2 * COLS, chan), BF16),
        in_specs=[vmem] * 14,
        out_specs=pl.BlockSpec(memory_space=pltpu.HBM),
        scratch_shapes=[
            pltpu.VMEM((side * PITCH + 8, chan), F32),
            pltpu.VMEM((side * PITCH, 3 * chan), BF16),
            pltpu.VMEM((inner, chan), BF16),
            pltpu.VMEM((3, ROWS * PITCH + 8, SPLIT), F32),
            pltpu.VMEM((chan // LANES, 2 * ROWS, 2 * COLS, LANES), F32),
            pltpu.VMEM((2 * ROWS, 2 * COLS, chan), BF16),
            pltpu.SemaphoreType.DMA((chan // SPLIT,)),
        ],
        compiler_params=pltpu.CompilerParams(vmem_limit_bytes=36 * 2**20),
        cost_estimate=pl.CostEstimate(
            flops=2_300_000_000, bytes_accessed=14_000_000, transcendentals=131_072
        ),
        name="decode_block",
    )(*args)


def shards(
    latent,
    gn_mean,
    gn_rstd,
    gn_gain,
    gn_shift,
    conv1_kernel,
    conv1_bias,
    conv2_kernel,
    conv2_bias,
    tile_dest,
):
    chan = latent.shape[2]
    full_rows = latent.shape[0] * lax.axis_size("img")
    full_cols = latent.shape[1] * lax.axis_size("bal")
    mesh_axes = ("img", "bal")
    core_pairs, even_pairs = pair_groups(lax.axis_size("img"), lax.axis_size("bal"))
    edge_core, edge_z = row_edges(latent, conv1_kernel, conv2_kernel)
    row_z = lax.ppermute(edge_z, "img", swaps(lax.axis_size("img"), 1))
    row_core = lax.all_gather(edge_core, mesh_axes, axis_index_groups=core_pairs)
    edge_odd, edge_even = column_edges(latent, row_z, row_core, conv1_kernel, conv2_kernel)
    col_odd = lax.ppermute(edge_odd, "bal", swaps(lax.axis_size("bal"), 1))
    col_even = lax.all_gather(edge_even, mesh_axes, axis_index_groups=even_pairs)
    return run_block(
        full_rows,
        full_cols,
        latent,
        row_z,
        row_core,
        col_odd,
        col_even,
        gn_mean.reshape(1, -1),
        gn_rstd.reshape(1, -1),
        gn_gain.reshape(1, chan),
        gn_shift.reshape(1, chan),
        conv1_kernel.reshape(3, 3 * chan, -1),
        conv1_bias.reshape(1, -1),
        conv2_kernel,
        conv2_bias.reshape(1, -1),
        tile_dest,
    )


def solution(mesh):
    placed = (P("img", "bal", None), P(), P(), P(), P(), P(), P(), P(), P(), P("img", "bal"))
    return jax.shard_map(
        shards, mesh=mesh, in_specs=placed, out_specs=P("img", "bal", None), check_vma=False
    )
```

```python
import functools

import jax
import jax.numpy as jnp
from jax import lax
from jax.experimental import pallas as pl
from jax.experimental.pallas import tpu as pltpu
from jax.sharding import PartitionSpec as P

TS = 3
TR = 4
TC = 4
ROWS = TR * TS
COLS = TC * TS
LANES = 128
SPLIT = 256
MARGIN = 8
PITCH = 16
F32 = jnp.float32
BF16 = jnp.bfloat16


def swaps(count, first):
    pairs = []
    for i in range(first, count - 1, 2):
        pairs += [(i, i + 1), (i + 1, i)]
    return pairs


def pair_groups(rows, cols):
    img = [[i * cols + j, (i + 1) * cols + j] for i in range(0, rows, 2) for j in range(cols)]
    bal = [[i * cols + j, i * cols + j + 1] for i in range(rows) for j in range(0, cols, 2)]
    return img, bal


def rows_kernel(x_hbm, w1_hbm, w2_hbm, core_ref, z_ref, sems):
    img_even = lax.axis_index("img") % 2 == 0
    last = x_hbm.shape[0] - 2
    core_at = jnp.where(img_even, last, 0)
    copies = [
        pltpu.make_async_copy(x_hbm.at[pl.ds(at, 2)], ref, sems.at[n])
        for n, (at, ref) in enumerate(((last - core_at, z_ref), (core_at, core_ref)))
    ]
    for copy in copies:
        copy.start()
    for copy in copies:
        copy.wait()


def row_edges(x, w1, w2):
    vmem = pl.BlockSpec(memory_space=pltpu.VMEM)
    edge = jax.ShapeDtypeStruct((2,) + x.shape[1:], BF16)
    return pl.pallas_call(
        rows_kernel,
        out_shape=(edge, edge),
        in_specs=[pl.BlockSpec(memory_space=pltpu.HBM)] * 3,
        out_specs=(vmem, vmem),
        scratch_shapes=[pltpu.SemaphoreType.DMA((2,))],
        compiler_params=pltpu.CompilerParams(vmem_limit_bytes=4 * 2**20),
        cost_estimate=pl.CostEstimate(flops=0, bytes_accessed=30_000_000, transcendentals=0),
        name="row_edges",
    )(*(pltpu.with_memory_space_constraint(a, pltpu.HBM) for a in (x, w1, w2)))


def columns_kernel(x_ref, row_z, row_core, w1_hbm, w2_hbm, odd_ref, even_ref):
    img_even = lax.axis_index("img") % 2 == 0
    bal_even = lax.axis_index("bal") % 2 == 0
    last = x_ref.shape[1]

    def put(row, cells):
        head, tail = cells[0:2], cells[last - 2 : last]
        odd_ref[row] = jnp.where(bal_even, head, tail)
        even_ref[row] = jnp.where(bal_even, tail, head)

    for r in range(2):
        put(r, jnp.where(img_even, row_z[r], row_core[0, r]))
        put(r + 2 + ROWS, jnp.where(img_even, row_core[1, r], row_z[r]))
    for r in range(ROWS):
        put(r + 2, x_ref[r])


def column_edges(x, row_z, row_core, w1, w2):
    vmem = pl.BlockSpec(memory_space=pltpu.VMEM)
    edge = jax.ShapeDtypeStruct((ROWS + 4, 2, x.shape[2]), BF16)
    return pl.pallas_call(
        columns_kernel,
        out_shape=(edge, edge),
        in_specs=[vmem] * 3 + [pl.BlockSpec(memory_space=pltpu.HBM)] * 2,
        out_specs=(vmem, vmem),
        compiler_params=pltpu.CompilerParams(vmem_limit_bytes=4 * 2**20),
        cost_estimate=pl.CostEstimate(flops=0, bytes_accessed=30_000_000, transcendentals=0),
        name="column_edges",
    )(x, row_z, row_core, *(pltpu.with_memory_space_constraint(a, pltpu.HBM) for a in (w1, w2)))


def block_kernel(
    full_rows,
    full_cols,
    x_ref,
    row_z,
    row_core,
    col_odd,
    col_even,
    mean_ref,
    rstd_ref,
    gain_ref,
    shift_ref,
    w1_ref,
    b1_ref,
    w2_ref,
    b2_ref,
    dest_ref,
    o_ref,
    act,
    taps,
    hid,
    wide,
    done,
    sems,
):
    chan = x_ref.shape[2]
    img = lax.axis_index("img")
    bal = lax.axis_index("bal")
    img_even = img % 2 == 0
    bal_even = bal % 2 == 0

    groups = mean_ref.shape[1]
    group_of = lax.broadcasted_iota(jnp.int32, (groups, chan), 1) // (chan // groups)
    spread = (lax.broadcasted_iota(jnp.int32, (groups, chan), 0) == group_of).astype(F32)
    exact = functools.partial(
        jnp.dot, precision=lax.Precision.HIGHEST, preferred_element_type=F32
    )
    mean = exact(jnp.broadcast_to(mean_ref[...], (8, groups)), spread)[0:1]
    rstd = exact(jnp.broadcast_to(rstd_ref[...], (8, groups)), spread)[0:1]
    gain = gain_ref[...]
    shift = shift_ref[...]

    scale = 0.5 * rstd * gain
    offset = 0.5 * shift - mean * scale

    def activate(cells):
        v = cells * scale + offset
        return v * jnp.tanh(v) + v

    side = ROWS + 4
    lines = [x_ref[r] for r in range(ROWS)]
    lines = [jnp.where(img_even, row_z[r], row_core[0, r]) for r in range(2)] + lines
    lines += [jnp.where(img_even, row_core[1, r], row_z[r]) for r in range(2)]
    for r, line in enumerate(lines):
        left = jnp.where(bal_even, col_odd[r], col_even[0, r])
        right = jnp.where(bal_even, col_even[1, r], col_odd[r])
        at = r * PITCH
        act[at : at + 2] = left.astype(F32)
        act[at + 2 : at + 2 + COLS] = line.astype(F32)
        act[at + 2 + COLS : at + PITCH] = right.astype(F32)
    cell = lax.broadcasted_iota(jnp.int32, (PITCH, 1), 0)
    col = bal * COLS - 2 + cell
    col_ok = (col >= 0) & (col < full_cols)
    for r in range(side):
        row = img * ROWS - 2 + r
        ok = col_ok & ((row >= 0) & (row < full_rows))
        at = slice(r * PITCH, (r + 1) * PITCH)
        act[at] = jnp.where(ok, activate(act[at]), 0.0)
    total = side * PITCH
    act[total:] = jnp.zeros((act.shape[0] - total, chan), F32)

    def shift(d):
        taps[:, d * chan : (d + 1) * chan] = act[d : d + total].astype(BF16)

    shift(0)

    inner = (ROWS + 2) * PITCH
    cell = lax.broadcasted_iota(jnp.int32, (inner, 1), 0)
    row = img * ROWS - 1 + cell // PITCH
    col = bal * COLS - 1 + cell % PITCH
    ok = (row >= 0) & (row < full_rows) & (col >= 0) & (col < full_cols)
    parts = [slice(n, n + SPLIT) for n in range(0, chan, SPLIT)]

    for part in parts:
        h = b1_ref[:, part]
        for e in range(3):
            lane = slice(e * chan, (e + 1) * chan)
            for d in range(3):
                h = h + jnp.dot(
                    taps[d * PITCH : d * PITCH + inner, lane],
                    w1_ref[d, lane, part],
                    preferred_element_type=F32,
                )
                if part.start == 0 and d == 0 and e < 2:
                    shift(e + 1)
        hid[:, part] = jnp.where(ok, h, 0.0).astype(BF16)

    cell = lax.broadcasted_iota(jnp.int32, (2 * COLS, TC), 0)
    own = cell // (2 * TS) == lax.broadcasted_iota(jnp.int32, (2 * COLS, TC), 1)
    live = [
        jnp.max(jnp.where(own, dest_ref[i : i + 1], -1), axis=1, keepdims=True) >= 0
        for i in range(TR)
    ]
    span = ROWS * PITCH
    met = ((0, PITCH + span), (PITCH, PITCH + span), (PITCH, 2 * PITCH + span))

    def finish(n, part, by_row):
        lanes = range(part.start // LANES, part.stop // LANES)
        bias = b2_ref[:, part]

        def row(p, r, sums):
            for m, (q, shift) in enumerate(((0, 0), (0, 1), (1, 1), (1, 2))):
                cells = sums[m][r * PITCH : (r + 1) * PITCH]
                at = pl.ds(MARGIN - 2 * shift + q, PITCH, stride=2)
                for lane, k in enumerate(lanes):
                    wide[m % 2, k, 2 * r + p, at] = cells[:, lane * LANES : (lane + 1) * LANES]
            for k in lanes:
                cells = wide[0, k, 2 * r + p, within] + wide[1, k, 2 * r + p, within]
                lane = slice(k * LANES, (k + 1) * LANES)
                done[2 * r + p, :, lane] = jnp.where(live[r // TS], cells, 0.0).astype(BF16)

        within = slice(MARGIN, MARGIN + 2 * COLS)
        for p in range(2):
            left, mid, right = by_row[p]
            mid = mid + bias
            sums = (left, mid + right, mid + left, right)
            for r in range(ROWS):
                yield functools.partial(row, p, r, sums)

    copies = []

    def send(n, part):
        copy = pltpu.make_async_copy(done.at[:, :, part], o_ref.at[:, :, part], sems.at[n])
        copy.start()
        copies.append(copy)

    steps = []
    for n, part in enumerate(parts):
        terms = {}
        turns = 9
        for turn in range(turns):
            dx, dy = divmod(turn, 3)
            a, b = met[dy]
            terms[dy, dx] = jnp.dot(hid[a:b], w2_ref[dy, dx, :, part], preferred_element_type=F32)
        by_row = [[], []]
        for dx in range(3):
            first, mid, last = (terms[dy, dx] for dy in range(3))
            by_row[0].append(first[:span] + (mid + last[:span]))
            by_row[1].append((first[PITCH:] + mid) + last[PITCH:])
        for step in finish(n, part, by_row):
            step()
        send(n, part)
    for copy in copies:
        copy.wait()


def run_block(full_rows, full_cols, *args):
    chan = args[0].shape[2]
    vmem = pl.BlockSpec(memory_space=pltpu.VMEM)
    side = ROWS + 4
    inner = (ROWS + 2) * PITCH
    return pl.pallas_call(
        functools.partial(block_kernel, full_rows, full_cols),
        out_shape=jax.ShapeDtypeStruct((2 * ROWS, 2 * COLS, chan), BF16),
        in_specs=[vmem] * 14,
        out_specs=pl.BlockSpec(memory_space=pltpu.HBM),
        scratch_shapes=[
            pltpu.VMEM((side * PITCH + 8, chan), F32),
            pltpu.VMEM((side * PITCH, 3 * chan), BF16),
            pltpu.VMEM((inner, chan), BF16),
            pltpu.VMEM((2, chan // LANES, 2 * ROWS, MARGIN + 2 * PITCH, LANES), F32),
            pltpu.VMEM((2 * ROWS, 2 * COLS, chan), BF16),
            pltpu.SemaphoreType.DMA((chan // SPLIT,)),
        ],
        compiler_params=pltpu.CompilerParams(vmem_limit_bytes=36 * 2**20),
        cost_estimate=pl.CostEstimate(
            flops=2_300_000_000, bytes_accessed=14_000_000, transcendentals=131_072
        ),
        name="decode_block",
    )(*args)


def shards(
    latent,
    gn_mean,
    gn_rstd,
    gn_gain,
    gn_shift,
    conv1_kernel,
    conv1_bias,
    conv2_kernel,
    conv2_bias,
    tile_dest,
):
    chan = latent.shape[2]
    full_rows = latent.shape[0] * lax.axis_size("img")
    full_cols = latent.shape[1] * lax.axis_size("bal")
    mesh_axes = ("img", "bal")
    core_pairs, even_pairs = pair_groups(lax.axis_size("img"), lax.axis_size("bal"))
    edge_core, edge_z = row_edges(latent, conv1_kernel, conv2_kernel)
    row_z = lax.ppermute(edge_z, "img", swaps(lax.axis_size("img"), 1))
    row_core = lax.all_gather(edge_core, mesh_axes, axis_index_groups=core_pairs)
    edge_odd, edge_even = column_edges(latent, row_z, row_core, conv1_kernel, conv2_kernel)
    col_odd = lax.ppermute(edge_odd, "bal", swaps(lax.axis_size("bal"), 1))
    col_even = lax.all_gather(edge_even, mesh_axes, axis_index_groups=even_pairs)
    return run_block(
        full_rows,
        full_cols,
        latent,
        row_z,
        row_core,
        col_odd,
        col_even,
        gn_mean.reshape(1, -1),
        gn_rstd.reshape(1, -1),
        gn_gain.reshape(1, chan),
        gn_shift.reshape(1, chan),
        conv1_kernel.reshape(3, 3 * chan, -1),
        conv1_bias.reshape(1, -1),
        conv2_kernel,
        conv2_bias.reshape(1, -1),
        tile_dest,
    )


def solution(mesh):
    placed = (P("img", "bal", None), P(), P(), P(), P(), P(), P(), P(), P(), P("img", "bal"))
    return jax.shard_map(
        shards, mesh=mesh, in_specs=placed, out_specs=P("img", "bal", None), check_vma=False
    )
```

```python
import functools

import jax
import jax.numpy as jnp
from jax import lax
from jax.experimental import pallas as pl
from jax.experimental.pallas import tpu as pltpu
from jax.sharding import PartitionSpec as P

TS = 3
TR = 4
TC = 4
ROWS = TR * TS
COLS = TC * TS
LANES = 128
SPLIT = 256
MARGIN = 8
PITCH = 16
F32 = jnp.float32
BF16 = jnp.bfloat16


def swaps(count, first):
    pairs = []
    for i in range(first, count - 1, 2):
        pairs += [(i, i + 1), (i + 1, i)]
    return pairs


def pair_groups(rows, cols):
    img = [[i * cols + j, (i + 1) * cols + j] for i in range(0, rows, 2) for j in range(cols)]
    bal = [[i * cols + j, i * cols + j + 1] for i in range(rows) for j in range(0, cols, 2)]
    return img, bal


def rows_kernel(x_hbm, core_ref, z_ref, sems):
    img_even = lax.axis_index("img") % 2 == 0
    last = x_hbm.shape[0] - 2
    core_at = jnp.where(img_even, last, 0)
    copies = [
        pltpu.make_async_copy(source, ref, sems.at[n])
        for n, (source, ref) in enumerate(
            (
                (x_hbm.at[pl.ds(last - core_at, 2)], z_ref),
                (x_hbm.at[pl.ds(core_at, 2)], core_ref),
            )
        )
    ]
    for copy in copies:
        copy.start()
    for copy in copies:
        copy.wait()


def row_edges(x):
    vmem = pl.BlockSpec(memory_space=pltpu.VMEM)
    edge = jax.ShapeDtypeStruct((2,) + x.shape[1:], BF16)
    return pl.pallas_call(
        rows_kernel,
        out_shape=(edge, edge),
        in_specs=[pl.BlockSpec(memory_space=pltpu.HBM)],
        out_specs=(vmem, vmem),
        scratch_shapes=[pltpu.SemaphoreType.DMA((2,))],
        compiler_params=pltpu.CompilerParams(vmem_limit_bytes=4 * 2**20),
        cost_estimate=pl.CostEstimate(flops=0, bytes_accessed=500_000, transcendentals=0),
        name="row_edges",
    )(pltpu.with_memory_space_constraint(x, pltpu.HBM))


def keep_kernel(edge_ref, *refs):
    refs[-1][...] = edge_ref[...]


def keep(edge, w1, w2):
    vmem = pl.BlockSpec(memory_space=pltpu.VMEM)
    return pl.pallas_call(
        keep_kernel,
        out_shape=jax.ShapeDtypeStruct(edge.shape, edge.dtype),
        in_specs=[vmem] + [pl.BlockSpec(memory_space=pltpu.HBM)] * 6,
        out_specs=vmem,
        compiler_params=pltpu.CompilerParams(vmem_limit_bytes=4 * 2**20),
        name="keep",
    )(edge, *(pltpu.with_memory_space_constraint(a, pltpu.HBM) for a in (w1, w2) * 3))


def columns_kernel(x_ref, row_z, row_core, odd_ref, even_ref):
    img_even = lax.axis_index("img") % 2 == 0
    bal_even = lax.axis_index("bal") % 2 == 0
    last = x_ref.shape[1]

    def put(row, cells):
        head, tail = cells[0:2], cells[last - 2 : last]
        odd_ref[row] = jnp.where(bal_even, head, tail)
        even_ref[row] = jnp.where(bal_even, tail, head)

    for r in range(2):
        put(r, jnp.where(img_even, row_z[r], row_core[0, r]))
        put(r + 2 + ROWS, jnp.where(img_even, row_core[1, r], row_z[r]))
    for r in range(ROWS):
        put(r + 2, x_ref[r])


def column_edges(x, row_z, row_core):
    vmem = pl.BlockSpec(memory_space=pltpu.VMEM)
    edge = jax.ShapeDtypeStruct((ROWS + 4, 2, x.shape[2]), BF16)
    return pl.pallas_call(
        columns_kernel,
        out_shape=(edge, edge),
        in_specs=[vmem] * 3,
        out_specs=(vmem, vmem),
        compiler_params=pltpu.CompilerParams(vmem_limit_bytes=4 * 2**20),
        cost_estimate=pl.CostEstimate(flops=0, bytes_accessed=30_000_000, transcendentals=0),
        name="column_edges",
    )(x, row_z, row_core)


def block_kernel(
    full_rows,
    full_cols,
    x_ref,
    row_z,
    row_core,
    col_odd,
    col_even,
    mean_ref,
    rstd_ref,
    gain_ref,
    shift_ref,
    w1_ref,
    b1_ref,
    w2_ref,
    b2_ref,
    dest_ref,
    o_ref,
    act,
    taps,
    hid,
    wide,
    done,
    sems,
):
    chan = x_ref.shape[2]
    img = lax.axis_index("img")
    bal = lax.axis_index("bal")
    img_even = img % 2 == 0
    bal_even = bal % 2 == 0

    groups = mean_ref.shape[1]
    group_of = lax.broadcasted_iota(jnp.int32, (groups, chan), 1) // (chan // groups)
    spread = (lax.broadcasted_iota(jnp.int32, (groups, chan), 0) == group_of).astype(F32)
    exact = functools.partial(
        jnp.dot, precision=lax.Precision.HIGHEST, preferred_element_type=F32
    )
    mean = exact(jnp.broadcast_to(mean_ref[...], (8, groups)), spread)[0:1]
    rstd = exact(jnp.broadcast_to(rstd_ref[...], (8, groups)), spread)[0:1]
    gain = gain_ref[...]
    shift = shift_ref[...]

    scale = 0.5 * rstd * gain
    offset = 0.5 * shift - mean * scale

    def activate(cells):
        v = cells * scale + offset
        return v * jnp.tanh(v) + v

    side = ROWS + 4
    lines = [x_ref[r] for r in range(ROWS)]
    lines = [jnp.where(img_even, row_z[r], row_core[0, r]) for r in range(2)] + lines
    lines += [jnp.where(img_even, row_core[1, r], row_z[r]) for r in range(2)]
    for r, line in enumerate(lines):
        left = jnp.where(bal_even, col_odd[r], col_even[0, r])
        right = jnp.where(bal_even, col_even[1, r], col_odd[r])
        at = r * PITCH
        act[at : at + 2] = left.astype(F32)
        act[at + 2 : at + 2 + COLS] = line.astype(F32)
        act[at + 2 + COLS : at + PITCH] = right.astype(F32)
    cell = lax.broadcasted_iota(jnp.int32, (PITCH, 1), 0)
    col = bal * COLS - 2 + cell
    col_ok = (col >= 0) & (col < full_cols)
    for r in range(side):
        row = img * ROWS - 2 + r
        ok = col_ok & ((row >= 0) & (row < full_rows))
        at = slice(r * PITCH, (r + 1) * PITCH)
        act[at] = jnp.where(ok, activate(act[at]), 0.0)
    total = side * PITCH
    act[total:] = jnp.zeros((act.shape[0] - total, chan), F32)

    def shift(d):
        taps[:, d * chan : (d + 1) * chan] = act[d : d + total].astype(BF16)

    shift(0)

    inner = (ROWS + 2) * PITCH
    cell = lax.broadcasted_iota(jnp.int32, (inner, 1), 0)
    row = img * ROWS - 1 + cell // PITCH
    col = bal * COLS - 1 + cell % PITCH
    ok = (row >= 0) & (row < full_rows) & (col >= 0) & (col < full_cols)
    parts = [slice(n, n + SPLIT) for n in range(0, chan, SPLIT)]

    for part in parts:
        h = b1_ref[:, part]
        for e in range(3):
            lane = slice(e * chan, (e + 1) * chan)
            for d in range(3):
                h = h + jnp.dot(
                    taps[d * PITCH : d * PITCH + inner, lane],
                    w1_ref[d, lane, part],
                    preferred_element_type=F32,
                )
                if part.start == 0 and d == 0 and e < 2:
                    shift(e + 1)
        hid[:, part] = jnp.where(ok, h, 0.0).astype(BF16)

    cell = lax.broadcasted_iota(jnp.int32, (2 * COLS, TC), 0)
    own = cell // (2 * TS) == lax.broadcasted_iota(jnp.int32, (2 * COLS, TC), 1)
    live = [
        jnp.max(jnp.where(own, dest_ref[i : i + 1], -1), axis=1, keepdims=True) >= 0
        for i in range(TR)
    ]
    span = ROWS * PITCH
    met = ((0, PITCH + span), (PITCH, PITCH + span), (PITCH, 2 * PITCH + span))

    def finish(n, part, by_row):
        lanes = range(part.start // LANES, part.stop // LANES)
        bias = b2_ref[:, part]

        def row(p, r, sums):
            for m, (q, shift) in enumerate(((0, 0), (0, 1), (1, 1), (1, 2))):
                cells = sums[m][r * PITCH : (r + 1) * PITCH]
                at = pl.ds(MARGIN - 2 * shift + q, PITCH, stride=2)
                for lane, k in enumerate(lanes):
                    wide[m % 2, k, 2 * r + p, at] = cells[:, lane * LANES : (lane + 1) * LANES]
            for k in lanes:
                cells = wide[0, k, 2 * r + p, within] + wide[1, k, 2 * r + p, within]
                lane = slice(k * LANES, (k + 1) * LANES)
                done[2 * r + p, :, lane] = jnp.where(live[r // TS], cells, 0.0).astype(BF16)

        within = slice(MARGIN, MARGIN + 2 * COLS)
        for p in range(2):
            left, mid, right = by_row[p]
            mid = mid + bias
            sums = (left, mid + right, mid + left, right)
            for r in range(ROWS):
                yield functools.partial(row, p, r, sums)

    copies = []

    def send(n, part):
        copy = pltpu.make_async_copy(done.at[:, :, part], o_ref.at[:, :, part], sems.at[n])
        copy.start()
        copies.append(copy)

    steps = []
    for n, part in enumerate(parts):
        terms = {}
        turns = 9
        for turn in range(turns):
            dx, dy = divmod(turn, 3)
            a, b = met[dy]
            terms[dy, dx] = jnp.dot(hid[a:b], w2_ref[dy, dx, :, part], preferred_element_type=F32)
        by_row = [[], []]
        for dx in range(3):
            first, mid, last = (terms[dy, dx] for dy in range(3))
            by_row[0].append(first[:span] + (mid + last[:span]))
            by_row[1].append((first[PITCH:] + mid) + last[PITCH:])
        for step in finish(n, part, by_row):
            step()
        send(n, part)
    for copy in copies:
        copy.wait()


def run_block(full_rows, full_cols, *args):
    chan = args[0].shape[2]
    vmem = pl.BlockSpec(memory_space=pltpu.VMEM)
    side = ROWS + 4
    inner = (ROWS + 2) * PITCH
    return pl.pallas_call(
        functools.partial(block_kernel, full_rows, full_cols),
        out_shape=jax.ShapeDtypeStruct((2 * ROWS, 2 * COLS, chan), BF16),
        in_specs=[vmem] * 14,
        out_specs=pl.BlockSpec(memory_space=pltpu.HBM),
        scratch_shapes=[
            pltpu.VMEM((side * PITCH + 8, chan), F32),
            pltpu.VMEM((side * PITCH, 3 * chan), BF16),
            pltpu.VMEM((inner, chan), BF16),
            pltpu.VMEM((2, chan // LANES, 2 * ROWS, MARGIN + 2 * PITCH, LANES), F32),
            pltpu.VMEM((2 * ROWS, 2 * COLS, chan), BF16),
            pltpu.SemaphoreType.DMA((chan // SPLIT,)),
        ],
        compiler_params=pltpu.CompilerParams(vmem_limit_bytes=36 * 2**20),
        cost_estimate=pl.CostEstimate(
            flops=2_300_000_000, bytes_accessed=14_000_000, transcendentals=131_072
        ),
        name="decode_block",
    )(*args)


def shards(
    latent,
    gn_mean,
    gn_rstd,
    gn_gain,
    gn_shift,
    conv1_kernel,
    conv1_bias,
    conv2_kernel,
    conv2_bias,
    tile_dest,
):
    chan = latent.shape[2]
    full_rows = latent.shape[0] * lax.axis_size("img")
    full_cols = latent.shape[1] * lax.axis_size("bal")
    mesh_axes = ("img", "bal")
    core_pairs, even_pairs = pair_groups(lax.axis_size("img"), lax.axis_size("bal"))
    edge_core, edge_z = row_edges(latent)
    row_z = lax.ppermute(edge_z, "img", swaps(lax.axis_size("img"), 1))
    edge_core = keep(edge_core, conv1_kernel, conv2_kernel)
    row_core = lax.all_gather(edge_core, mesh_axes, axis_index_groups=core_pairs)
    edge_odd, edge_even = column_edges(latent, row_z, row_core)
    col_odd = lax.ppermute(edge_odd, "bal", swaps(lax.axis_size("bal"), 1))
    col_even = lax.all_gather(edge_even, mesh_axes, axis_index_groups=even_pairs)
    return run_block(
        full_rows,
        full_cols,
        latent,
        row_z,
        row_core,
        col_odd,
        col_even,
        gn_mean.reshape(1, -1),
        gn_rstd.reshape(1, -1),
        gn_gain.reshape(1, chan),
        gn_shift.reshape(1, chan),
        conv1_kernel.reshape(3, 3 * chan, -1),
        conv1_bias.reshape(1, -1),
        conv2_kernel,
        conv2_bias.reshape(1, -1),
        tile_dest,
    )


def solution(mesh):
    placed = (P("img", "bal", None), P(), P(), P(), P(), P(), P(), P(), P(), P("img", "bal"))
    return jax.shard_map(
        shards, mesh=mesh, in_specs=placed, out_specs=P("img", "bal", None), check_vma=False
    )
```

```python
import functools

import jax
import jax.numpy as jnp
from jax import lax
from jax.experimental import pallas as pl
from jax.experimental.pallas import tpu as pltpu
from jax.sharding import PartitionSpec as P

TS = 3
TR = 4
TC = 4
ROWS = TR * TS
COLS = TC * TS
LANES = 128
SPLIT = 256
MARGIN = 8
PITCH = 16
F32 = jnp.float32
BF16 = jnp.bfloat16


def swaps(count, first):
    pairs = []
    for i in range(first, count - 1, 2):
        pairs += [(i, i + 1), (i + 1, i)]
    return pairs


def pair_groups(rows, cols):
    img = [[i * cols + j, (i + 1) * cols + j] for i in range(0, rows, 2) for j in range(cols)]
    bal = [[i * cols + j, i * cols + j + 1] for i in range(rows) for j in range(0, cols, 2)]
    return img, bal


def rows_kernel(x_hbm, core_ref, z_ref, sems):
    img_even = lax.axis_index("img") % 2 == 0
    last = x_hbm.shape[0] - 2
    core_at = jnp.where(img_even, last, 0)
    copies = [
        pltpu.make_async_copy(source, ref, sems.at[n])
        for n, (source, ref) in enumerate(
            (
                (x_hbm.at[pl.ds(last - core_at, 2)], z_ref),
                (x_hbm.at[pl.ds(core_at, 2)], core_ref),
            )
        )
    ]
    for copy in copies:
        copy.start()
    for copy in copies:
        copy.wait()


def row_edges(x):
    vmem = pl.BlockSpec(memory_space=pltpu.VMEM)
    edge = jax.ShapeDtypeStruct((2,) + x.shape[1:], BF16)
    return pl.pallas_call(
        rows_kernel,
        out_shape=(edge, edge),
        in_specs=[pl.BlockSpec(memory_space=pltpu.HBM)],
        out_specs=(vmem, vmem),
        scratch_shapes=[pltpu.SemaphoreType.DMA((2,))],
        compiler_params=pltpu.CompilerParams(vmem_limit_bytes=4 * 2**20),
        cost_estimate=pl.CostEstimate(flops=0, bytes_accessed=500_000, transcendentals=0),
        name="row_edges",
    )(pltpu.with_memory_space_constraint(x, pltpu.HBM))


def keep_kernel(edge_ref, *refs):
    refs[-1][...] = edge_ref[...]


def keep(edge, w1, w2):
    vmem = pl.BlockSpec(memory_space=pltpu.VMEM)
    return pl.pallas_call(
        keep_kernel,
        out_shape=jax.ShapeDtypeStruct(edge.shape, edge.dtype),
        in_specs=[vmem] + [pl.BlockSpec(memory_space=pltpu.HBM)] * 6,
        out_specs=vmem,
        compiler_params=pltpu.CompilerParams(vmem_limit_bytes=4 * 2**20),
        name="keep",
    )(edge, *(pltpu.with_memory_space_constraint(a, pltpu.HBM) for a in (w1, w2) * 3))


def columns_kernel(x_ref, row_z, row_core, odd_ref, even_ref):
    img_even = lax.axis_index("img") % 2 == 0
    bal_even = lax.axis_index("bal") % 2 == 0
    last = x_ref.shape[1]

    def put(row, cells):
        head, tail = cells[0:2], cells[last - 2 : last]
        odd_ref[row] = jnp.where(bal_even, head, tail)
        even_ref[row] = jnp.where(bal_even, tail, head)

    for r in range(2):
        put(r, jnp.where(img_even, row_z[r], row_core[0, r]))
        put(r + 2 + ROWS, jnp.where(img_even, row_core[1, r], row_z[r]))
    for r in range(ROWS):
        put(r + 2, x_ref[r])


def column_edges(x, row_z, row_core):
    vmem = pl.BlockSpec(memory_space=pltpu.VMEM)
    edge = jax.ShapeDtypeStruct((ROWS + 4, 2, x.shape[2]), BF16)
    return pl.pallas_call(
        columns_kernel,
        out_shape=(edge, edge),
        in_specs=[vmem] * 3,
        out_specs=(vmem, vmem),
        compiler_params=pltpu.CompilerParams(vmem_limit_bytes=4 * 2**20),
        cost_estimate=pl.CostEstimate(flops=0, bytes_accessed=30_000_000, transcendentals=0),
        name="column_edges",
    )(x, row_z, row_core)


def block_kernel(
    full_rows,
    full_cols,
    x_ref,
    row_z,
    row_core,
    col_odd,
    col_even,
    mean_ref,
    rstd_ref,
    gain_ref,
    shift_ref,
    w1_ref,
    b1_ref,
    w2_ref,
    b2_ref,
    dest_ref,
    o_ref,
    act,
    taps,
    hid,
    wide,
    done,
    sems,
):
    chan = x_ref.shape[2]
    img = lax.axis_index("img")
    bal = lax.axis_index("bal")
    img_even = img % 2 == 0
    bal_even = bal % 2 == 0

    groups = mean_ref.shape[1]
    group_of = lax.broadcasted_iota(jnp.int32, (groups, chan), 1) // (chan // groups)
    spread = (lax.broadcasted_iota(jnp.int32, (groups, chan), 0) == group_of).astype(F32)
    exact = functools.partial(
        jnp.dot, precision=lax.Precision.HIGHEST, preferred_element_type=F32
    )
    mean = exact(jnp.broadcast_to(mean_ref[...], (8, groups)), spread)[0:1]
    rstd = exact(jnp.broadcast_to(rstd_ref[...], (8, groups)), spread)[0:1]
    gain = gain_ref[...]
    shift = shift_ref[...]

    scale = 0.5 * rstd * gain
    offset = 0.5 * shift - mean * scale

    def activate(cells):
        v = cells * scale + offset
        return v * jnp.tanh(v) + v

    side = ROWS + 4
    lines = [x_ref[r] for r in range(ROWS)]
    lines = [jnp.where(img_even, row_z[r], row_core[0, r]) for r in range(2)] + lines
    lines += [jnp.where(img_even, row_core[1, r], row_z[r]) for r in range(2)]
    for r, line in enumerate(lines):
        left = jnp.where(bal_even, col_odd[r], col_even[0, r])
        right = jnp.where(bal_even, col_even[1, r], col_odd[r])
        at = r * PITCH
        act[at : at + 2] = left.astype(F32)
        act[at + 2 : at + 2 + COLS] = line.astype(F32)
        act[at + 2 + COLS : at + PITCH] = right.astype(F32)
    cell = lax.broadcasted_iota(jnp.int32, (PITCH, 1), 0)
    col = bal * COLS - 2 + cell
    col_ok = (col >= 0) & (col < full_cols)
    for r in range(side):
        row = img * ROWS - 2 + r
        ok = col_ok & ((row >= 0) & (row < full_rows))
        at = slice(r * PITCH, (r + 1) * PITCH)
        act[at] = jnp.where(ok, activate(act[at]), 0.0)
    total = side * PITCH
    act[total:] = jnp.zeros((act.shape[0] - total, chan), F32)

    for d in range(3):
        taps[:, d * chan : (d + 1) * chan] = act[d : d + total].astype(BF16)

    inner = (ROWS + 2) * PITCH
    cell = lax.broadcasted_iota(jnp.int32, (inner, 1), 0)
    row = img * ROWS - 1 + cell // PITCH
    col = bal * COLS - 1 + cell % PITCH
    ok = (row >= 0) & (row < full_rows) & (col >= 0) & (col < full_cols)
    parts = [slice(n, n + SPLIT) for n in range(0, chan, SPLIT)]

    for part in parts:
        h = b1_ref[:, part]
        for d in range(3):
            h = h + jnp.dot(
                taps[d * PITCH : d * PITCH + inner], w1_ref[d, :, part], preferred_element_type=F32
            )
        hid[:, part] = jnp.where(ok, h, 0.0).astype(BF16)

    cell = lax.broadcasted_iota(jnp.int32, (2 * COLS, TC), 0)
    own = cell // (2 * TS) == lax.broadcasted_iota(jnp.int32, (2 * COLS, TC), 1)
    live = [
        jnp.max(jnp.where(own, dest_ref[i : i + 1], -1), axis=1, keepdims=True) >= 0
        for i in range(TR)
    ]
    span = ROWS * PITCH
    met = ((0, PITCH + span), (PITCH, PITCH + span), (PITCH, 2 * PITCH + span))

    within = slice(MARGIN, MARGIN + 2 * COLS)
    copies = []
    for n, part in enumerate(parts):
        lanes = range(part.start // LANES, part.stop // LANES)
        bias = b2_ref[:, part]

        def scatter(side, p, q, shift, sums):
            at = pl.ds(MARGIN - 2 * shift + q, PITCH, stride=2)
            for r in range(ROWS):
                cells = sums[r * PITCH : (r + 1) * PITCH]
                for lane, k in enumerate(lanes):
                    wide[side, k, 2 * r + p, at] = cells[:, lane * LANES : (lane + 1) * LANES]

        by_row = []
        for dx in range(3):
            first, mid, last = (
                jnp.dot(hid[a:b], w2_ref[dy, dx, :, part], preferred_element_type=F32)
                for dy, (a, b) in enumerate(met)
            )
            if dx == 1:
                mid = mid + bias
            by_row.append((first[:span] + (mid + last[:span]), (first[PITCH:] + mid) + last[PITCH:]))
            for p in range(2):
                if dx == 0:
                    scatter(0, p, 0, 0, by_row[0][p])
                elif dx == 1:
                    scatter(0, p, 1, 1, by_row[0][p] + by_row[1][p])
                else:
                    scatter(1, p, 0, 1, by_row[1][p] + by_row[2][p])
                    scatter(1, p, 1, 2, by_row[2][p])
        for row in range(2 * ROWS):
            for k in lanes:
                cells = wide[0, k, row, within] + wide[1, k, row, within]
                lane = slice(k * LANES, (k + 1) * LANES)
                done[row, :, lane] = jnp.where(live[row // (2 * TS)], cells, 0.0).astype(BF16)
        copy = pltpu.make_async_copy(done.at[:, :, part], o_ref.at[:, :, part], sems.at[n])
        copy.start()
        copies.append(copy)
    for copy in copies:
        copy.wait()


def run_block(full_rows, full_cols, *args):
    chan = args[0].shape[2]
    vmem = pl.BlockSpec(memory_space=pltpu.VMEM)
    side = ROWS + 4
    inner = (ROWS + 2) * PITCH
    return pl.pallas_call(
        functools.partial(block_kernel, full_rows, full_cols),
        out_shape=jax.ShapeDtypeStruct((2 * ROWS, 2 * COLS, chan), BF16),
        in_specs=[vmem] * 14,
        out_specs=pl.BlockSpec(memory_space=pltpu.HBM),
        scratch_shapes=[
            pltpu.VMEM((side * PITCH + 8, chan), F32),
            pltpu.VMEM((side * PITCH, 3 * chan), BF16),
            pltpu.VMEM((inner, chan), BF16),
            pltpu.VMEM((2, chan // LANES, 2 * ROWS, MARGIN + 2 * PITCH, LANES), F32),
            pltpu.VMEM((2 * ROWS, 2 * COLS, chan), BF16),
            pltpu.SemaphoreType.DMA((chan // SPLIT,)),
        ],
        compiler_params=pltpu.CompilerParams(vmem_limit_bytes=36 * 2**20),
        cost_estimate=pl.CostEstimate(
            flops=2_300_000_000, bytes_accessed=14_000_000, transcendentals=131_072
        ),
        name="decode_block",
    )(*args)


def shards(
    latent,
    gn_mean,
    gn_rstd,
    gn_gain,
    gn_shift,
    conv1_kernel,
    conv1_bias,
    conv2_kernel,
    conv2_bias,
    tile_dest,
):
    chan = latent.shape[2]
    full_rows = latent.shape[0] * lax.axis_size("img")
    full_cols = latent.shape[1] * lax.axis_size("bal")
    mesh_axes = ("img", "bal")
    core_pairs, even_pairs = pair_groups(lax.axis_size("img"), lax.axis_size("bal"))
    edge_core, edge_z = row_edges(latent)
    row_z = lax.ppermute(edge_z, "img", swaps(lax.axis_size("img"), 1))
    edge_core = keep(edge_core, conv1_kernel, conv2_kernel)
    row_core = lax.all_gather(edge_core, mesh_axes, axis_index_groups=core_pairs)
    edge_odd, edge_even = column_edges(latent, row_z, row_core)
    col_odd = lax.ppermute(edge_odd, "bal", swaps(lax.axis_size("bal"), 1))
    col_even = lax.all_gather(edge_even, mesh_axes, axis_index_groups=even_pairs)
    return run_block(
        full_rows,
        full_cols,
        latent,
        row_z,
        row_core,
        col_odd,
        col_even,
        gn_mean.reshape(1, -1),
        gn_rstd.reshape(1, -1),
        gn_gain.reshape(1, chan),
        gn_shift.reshape(1, chan),
        conv1_kernel.reshape(3, 3 * chan, -1),
        conv1_bias.reshape(1, -1),
        conv2_kernel,
        conv2_bias.reshape(1, -1),
        tile_dest,
    )


def solution(mesh):
    placed = (P("img", "bal", None), P(), P(), P(), P(), P(), P(), P(), P(), P("img", "bal"))
    return jax.shard_map(
        shards, mesh=mesh, in_specs=placed, out_specs=P("img", "bal", None), check_vma=False
    )
```

```python
import functools

import jax
import jax.numpy as jnp
from jax import lax
from jax.experimental import pallas as pl
from jax.experimental.pallas import tpu as pltpu
from jax.sharding import PartitionSpec as P

TS = 3
TR = 4
TC = 4
ROWS = TR * TS
COLS = TC * TS
LANES = 128
SPLIT = 256
BATCH = 12
MARGIN = 8
PITCH = 16
F32 = jnp.float32
BF16 = jnp.bfloat16


def swaps(count, first):
    pairs = []
    for i in range(first, count - 1, 2):
        pairs += [(i, i + 1), (i + 1, i)]
    return pairs


def pair_groups(rows, cols):
    img = [[i * cols + j, (i + 1) * cols + j] for i in range(0, rows, 2) for j in range(cols)]
    bal = [[i * cols + j, i * cols + j + 1] for i in range(rows) for j in range(0, cols, 2)]
    return img, bal


def rows_kernel(x_hbm, core_ref, z_ref, sems):
    img_even = lax.axis_index("img") % 2 == 0
    last = x_hbm.shape[0] - 2
    core_at = jnp.where(img_even, last, 0)
    copies = [
        pltpu.make_async_copy(source, ref, sems.at[n])
        for n, (source, ref) in enumerate(
            (
                (x_hbm.at[pl.ds(last - core_at, 2)], z_ref),
                (x_hbm.at[pl.ds(core_at, 2)], core_ref),
            )
        )
    ]
    for copy in copies:
        copy.start()
    for copy in copies:
        copy.wait()


def row_edges(x):
    vmem = pl.BlockSpec(memory_space=pltpu.VMEM)
    edge = jax.ShapeDtypeStruct((2,) + x.shape[1:], BF16)
    return pl.pallas_call(
        rows_kernel,
        out_shape=(edge, edge),
        in_specs=[pl.BlockSpec(memory_space=pltpu.HBM)],
        out_specs=(vmem, vmem),
        scratch_shapes=[pltpu.SemaphoreType.DMA((2,))],
        compiler_params=pltpu.CompilerParams(vmem_limit_bytes=4 * 2**20),
        cost_estimate=pl.CostEstimate(flops=0, bytes_accessed=500_000, transcendentals=0),
        name="row_edges",
    )(pltpu.with_memory_space_constraint(x, pltpu.HBM))


def keep_kernel(edge_ref, *refs):
    refs[-1][...] = edge_ref[...]


def keep(edge, w1, w2):
    vmem = pl.BlockSpec(memory_space=pltpu.VMEM)
    return pl.pallas_call(
        keep_kernel,
        out_shape=jax.ShapeDtypeStruct(edge.shape, edge.dtype),
        in_specs=[vmem] + [pl.BlockSpec(memory_space=pltpu.HBM)] * 6,
        out_specs=vmem,
        compiler_params=pltpu.CompilerParams(vmem_limit_bytes=4 * 2**20),
        name="keep",
    )(edge, *(pltpu.with_memory_space_constraint(a, pltpu.HBM) for a in (w1, w2) * 3))


def columns_kernel(x_ref, row_z, row_core, odd_ref, even_ref):
    img_even = lax.axis_index("img") % 2 == 0
    bal_even = lax.axis_index("bal") % 2 == 0
    last = x_ref.shape[1]

    def put(row, cells):
        head, tail = cells[0:2], cells[last - 2 : last]
        odd_ref[row] = jnp.where(bal_even, head, tail)
        even_ref[row] = jnp.where(bal_even, tail, head)

    for r in range(2):
        put(r, jnp.where(img_even, row_z[r], row_core[0, r]))
        put(r + 2 + ROWS, jnp.where(img_even, row_core[1, r], row_z[r]))
    for r in range(ROWS):
        put(r + 2, x_ref[r])


def column_edges(x, row_z, row_core):
    vmem = pl.BlockSpec(memory_space=pltpu.VMEM)
    edge = jax.ShapeDtypeStruct((ROWS + 4, 2, x.shape[2]), BF16)
    return pl.pallas_call(
        columns_kernel,
        out_shape=(edge, edge),
        in_specs=[vmem] * 3,
        out_specs=(vmem, vmem),
        compiler_params=pltpu.CompilerParams(vmem_limit_bytes=4 * 2**20),
        cost_estimate=pl.CostEstimate(flops=0, bytes_accessed=30_000_000, transcendentals=0),
        name="column_edges",
    )(x, row_z, row_core)


def block_kernel(
    full_rows,
    full_cols,
    x_ref,
    row_z,
    row_core,
    col_odd,
    col_even,
    mean_ref,
    rstd_ref,
    gain_ref,
    shift_ref,
    w1_ref,
    b1_ref,
    w2_ref,
    b2_ref,
    dest_ref,
    o_ref,
    act,
    taps,
    hid,
    wide,
    done,
    sems,
):
    chan = x_ref.shape[2]
    img = lax.axis_index("img")
    bal = lax.axis_index("bal")
    img_even = img % 2 == 0
    bal_even = bal % 2 == 0

    groups = mean_ref.shape[1]
    group_of = lax.broadcasted_iota(jnp.int32, (groups, chan), 1) // (chan // groups)
    spread = (lax.broadcasted_iota(jnp.int32, (groups, chan), 0) == group_of).astype(F32)
    exact = functools.partial(
        jnp.dot, precision=lax.Precision.HIGHEST, preferred_element_type=F32
    )
    mean = exact(jnp.broadcast_to(mean_ref[...], (8, groups)), spread)[0:1]
    rstd = exact(jnp.broadcast_to(rstd_ref[...], (8, groups)), spread)[0:1]
    gain = gain_ref[...]
    shift = shift_ref[...]

    scale = 0.5 * rstd * gain
    offset = 0.5 * shift - mean * scale

    def activate(cells):
        v = cells * scale + offset
        return v * jnp.tanh(v) + v

    side = ROWS + 4
    lines = [x_ref[r] for r in range(ROWS)]
    lines = [jnp.where(img_even, row_z[r], row_core[0, r]) for r in range(2)] + lines
    lines += [jnp.where(img_even, row_core[1, r], row_z[r]) for r in range(2)]
    for r, line in enumerate(lines):
        left = jnp.where(bal_even, col_odd[r], col_even[0, r])
        right = jnp.where(bal_even, col_even[1, r], col_odd[r])
        at = r * PITCH
        act[at : at + 2] = left.astype(F32)
        act[at + 2 : at + 2 + COLS] = line.astype(F32)
        act[at + 2 + COLS : at + PITCH] = right.astype(F32)
    cell = lax.broadcasted_iota(jnp.int32, (PITCH, 1), 0)
    col = bal * COLS - 2 + cell
    col_ok = (col >= 0) & (col < full_cols)
    for r in range(side):
        row = img * ROWS - 2 + r
        ok = col_ok & ((row >= 0) & (row < full_rows))
        at = slice(r * PITCH, (r + 1) * PITCH)
        act[at] = jnp.where(ok, activate(act[at]), 0.0)
    total = side * PITCH
    act[total:] = jnp.zeros((act.shape[0] - total, chan), F32)

    for d in range(3):
        taps[:, d * chan : (d + 1) * chan] = act[d : d + total].astype(BF16)

    inner = (ROWS + 2) * PITCH
    cell = lax.broadcasted_iota(jnp.int32, (inner, 1), 0)
    row = img * ROWS - 1 + cell // PITCH
    col = bal * COLS - 1 + cell % PITCH
    ok = (row >= 0) & (row < full_rows) & (col >= 0) & (col < full_cols)
    parts = [slice(n, n + SPLIT) for n in range(0, chan, SPLIT)]

    for part in parts:
        h = b1_ref[:, part]
        for d in range(3):
            h = h + jnp.dot(
                taps[d * PITCH : d * PITCH + inner], w1_ref[d, :, part], preferred_element_type=F32
            )
        hid[:, part] = jnp.where(ok, h, 0.0).astype(BF16)

    cell = lax.broadcasted_iota(jnp.int32, (2 * COLS, TC), 0)
    own = cell // (2 * TS) == lax.broadcasted_iota(jnp.int32, (2 * COLS, TC), 1)
    live = [
        jnp.max(jnp.where(own, dest_ref[i : i + 1], -1), axis=1, keepdims=True) >= 0
        for i in range(TR)
    ]
    span = ROWS * PITCH
    met = ((0, PITCH + span), (PITCH, PITCH + span), (PITCH, 2 * PITCH + span))

    within = slice(MARGIN, MARGIN + 2 * COLS)
    copies = []
    for n, part in enumerate(parts):
        lanes = range(part.start // LANES, part.stop // LANES)
        bias = b2_ref[:, part]

        def scatter(side, p, q, shift, sums):
            at = pl.ds(MARGIN - 2 * shift + q, PITCH, stride=2)
            for r in range(ROWS):
                cells = sums[r * PITCH : (r + 1) * PITCH]
                for lane, k in enumerate(lanes):
                    wide[side, k, 2 * r + p, at] = cells[:, lane * LANES : (lane + 1) * LANES]

        by_row = []
        for dx in range(3):
            first, mid, last = (
                jnp.dot(hid[a:b], w2_ref[dy, dx, :, part], preferred_element_type=F32)
                for dy, (a, b) in enumerate(met)
            )
            if dx == 1:
                mid = mid + bias
            by_row.append((first[:span] + (mid + last[:span]), (first[PITCH:] + mid) + last[PITCH:]))
            for p in range(2):
                if dx == 0:
                    scatter(0, p, 0, 0, by_row[0][p])
                elif dx == 1:
                    scatter(0, p, 1, 1, by_row[0][p] + by_row[1][p])
                else:
                    scatter(1, p, 0, 1, by_row[1][p] + by_row[2][p])
                    scatter(1, p, 1, 2, by_row[2][p])
        for row in range(2 * ROWS):
            for k in lanes:
                cells = wide[0, k, row, within] + wide[1, k, row, within]
                lane = slice(k * LANES, (k + 1) * LANES)
                done[row, :, lane] = jnp.where(live[row // (2 * TS)], cells, 0.0).astype(BF16)
            if (row + 1) % BATCH == 0:
                at = (slice(row + 1 - BATCH, row + 1), slice(None), part)
                copy = pltpu.make_async_copy(done.at[at], o_ref.at[at], sems.at[len(copies)])
                copy.start()
                copies.append(copy)
    for copy in copies:
        copy.wait()


def run_block(full_rows, full_cols, *args):
    chan = args[0].shape[2]
    vmem = pl.BlockSpec(memory_space=pltpu.VMEM)
    side = ROWS + 4
    inner = (ROWS + 2) * PITCH
    return pl.pallas_call(
        functools.partial(block_kernel, full_rows, full_cols),
        out_shape=jax.ShapeDtypeStruct((2 * ROWS, 2 * COLS, chan), BF16),
        in_specs=[vmem] * 14,
        out_specs=pl.BlockSpec(memory_space=pltpu.HBM),
        scratch_shapes=[
            pltpu.VMEM((side * PITCH + 8, chan), F32),
            pltpu.VMEM((side * PITCH, 3 * chan), BF16),
            pltpu.VMEM((inner, chan), BF16),
            pltpu.VMEM((2, chan // LANES, 2 * ROWS, MARGIN + 2 * PITCH, LANES), F32),
            pltpu.VMEM((2 * ROWS, 2 * COLS, chan), BF16),
            pltpu.SemaphoreType.DMA((chan // SPLIT * 2 * ROWS // BATCH,)),
        ],
        compiler_params=pltpu.CompilerParams(vmem_limit_bytes=36 * 2**20),
        cost_estimate=pl.CostEstimate(
            flops=2_300_000_000, bytes_accessed=14_000_000, transcendentals=131_072
        ),
        name="decode_block",
    )(*args)


def shards(
    latent,
    gn_mean,
    gn_rstd,
    gn_gain,
    gn_shift,
    conv1_kernel,
    conv1_bias,
    conv2_kernel,
    conv2_bias,
    tile_dest,
):
    chan = latent.shape[2]
    full_rows = latent.shape[0] * lax.axis_size("img")
    full_cols = latent.shape[1] * lax.axis_size("bal")
    mesh_axes = ("img", "bal")
    core_pairs, even_pairs = pair_groups(lax.axis_size("img"), lax.axis_size("bal"))
    edge_core, edge_z = row_edges(latent)
    row_z = lax.ppermute(edge_z, "img", swaps(lax.axis_size("img"), 1))
    edge_core = keep(edge_core, conv1_kernel, conv2_kernel)
    row_core = lax.all_gather(edge_core, mesh_axes, axis_index_groups=core_pairs)
    edge_odd, edge_even = column_edges(latent, row_z, row_core)
    col_odd = lax.ppermute(edge_odd, "bal", swaps(lax.axis_size("bal"), 1))
    col_even = lax.all_gather(edge_even, mesh_axes, axis_index_groups=even_pairs)
    return run_block(
        full_rows,
        full_cols,
        latent,
        row_z,
        row_core,
        col_odd,
        col_even,
        gn_mean.reshape(1, -1),
        gn_rstd.reshape(1, -1),
        gn_gain.reshape(1, chan),
        gn_shift.reshape(1, chan),
        conv1_kernel.reshape(3, 3 * chan, -1),
        conv1_bias.reshape(1, -1),
        conv2_kernel,
        conv2_bias.reshape(1, -1),
        tile_dest,
    )


def solution(mesh):
    placed = (P("img", "bal", None), P(), P(), P(), P(), P(), P(), P(), P(), P("img", "bal"))
    return jax.shard_map(
        shards, mesh=mesh, in_specs=placed, out_specs=P("img", "bal", None), check_vma=False
    )
```

```python
import functools

import jax
import jax.numpy as jnp
from jax import lax
from jax.experimental import pallas as pl
from jax.experimental.pallas import tpu as pltpu
from jax.sharding import PartitionSpec as P

TS = 3
TR = 4
TC = 4
ROWS = TR * TS
COLS = TC * TS
LANES = 128
SPLIT = 256
BATCH = 12
MARGIN = 8
PITCH = 16
F32 = jnp.float32
BF16 = jnp.bfloat16


def swaps(count, first):
    pairs = []
    for i in range(first, count - 1, 2):
        pairs += [(i, i + 1), (i + 1, i)]
    return pairs


def pair_groups(rows, cols):
    img = [[i * cols + j, (i + 1) * cols + j] for i in range(0, rows, 2) for j in range(cols)]
    bal = [[i * cols + j, i * cols + j + 1] for i in range(rows) for j in range(0, cols, 2)]
    return img, bal


def rows_kernel(x_hbm, core_ref, z_ref, sems):
    img_even = lax.axis_index("img") % 2 == 0
    last = x_hbm.shape[0] - 2
    core_at = jnp.where(img_even, last, 0)
    copies = [
        pltpu.make_async_copy(source, ref, sems.at[n])
        for n, (source, ref) in enumerate(
            (
                (x_hbm.at[pl.ds(last - core_at, 2)], z_ref),
                (x_hbm.at[pl.ds(core_at, 2)], core_ref),
            )
        )
    ]
    for copy in copies:
        copy.start()
    for copy in copies:
        copy.wait()


def row_edges(x):
    vmem = pl.BlockSpec(memory_space=pltpu.VMEM)
    edge = jax.ShapeDtypeStruct((2,) + x.shape[1:], BF16)
    return pl.pallas_call(
        rows_kernel,
        out_shape=(edge, edge),
        in_specs=[pl.BlockSpec(memory_space=pltpu.HBM)],
        out_specs=(vmem, vmem),
        scratch_shapes=[pltpu.SemaphoreType.DMA((2,))],
        compiler_params=pltpu.CompilerParams(vmem_limit_bytes=4 * 2**20),
        cost_estimate=pl.CostEstimate(flops=0, bytes_accessed=500_000, transcendentals=0),
        name="row_edges",
    )(pltpu.with_memory_space_constraint(x, pltpu.HBM))


def keep_kernel(edge_ref, *refs):
    refs[-1][...] = edge_ref[...]


def keep(edge, w1, w2):
    vmem = pl.BlockSpec(memory_space=pltpu.VMEM)
    return pl.pallas_call(
        keep_kernel,
        out_shape=jax.ShapeDtypeStruct(edge.shape, edge.dtype),
        in_specs=[vmem] + [pl.BlockSpec(memory_space=pltpu.HBM)] * 6,
        out_specs=vmem,
        compiler_params=pltpu.CompilerParams(vmem_limit_bytes=4 * 2**20),
        name="keep",
    )(edge, *(pltpu.with_memory_space_constraint(a, pltpu.HBM) for a in (w1, w2) * 3))


def columns_kernel(x_ref, row_z, row_core, odd_ref, even_ref):
    img_even = lax.axis_index("img") % 2 == 0
    bal_even = lax.axis_index("bal") % 2 == 0
    last = x_ref.shape[1]

    def put(row, cells):
        head, tail = cells[0:2], cells[last - 2 : last]
        odd_ref[row] = jnp.where(bal_even, head, tail)
        even_ref[row] = jnp.where(bal_even, tail, head)

    for r in range(2):
        put(r, jnp.where(img_even, row_z[r], row_core[0, r]))
        put(r + 2 + ROWS, jnp.where(img_even, row_core[1, r], row_z[r]))
    for r in range(ROWS):
        put(r + 2, x_ref[r])


def column_edges(x, row_z, row_core):
    vmem = pl.BlockSpec(memory_space=pltpu.VMEM)
    edge = jax.ShapeDtypeStruct((ROWS + 4, 2, x.shape[2]), BF16)
    return pl.pallas_call(
        columns_kernel,
        out_shape=(edge, edge),
        in_specs=[vmem] * 3,
        out_specs=(vmem, vmem),
        compiler_params=pltpu.CompilerParams(vmem_limit_bytes=4 * 2**20),
        cost_estimate=pl.CostEstimate(flops=0, bytes_accessed=30_000_000, transcendentals=0),
        name="column_edges",
    )(x, row_z, row_core)


def block_kernel(
    full_rows,
    full_cols,
    x_ref,
    row_z,
    row_core,
    col_odd,
    col_even,
    mean_ref,
    rstd_ref,
    gain_ref,
    shift_ref,
    w1_ref,
    b1_ref,
    w2_ref,
    b2_ref,
    dest_ref,
    o_ref,
    act,
    taps,
    hid,
    wide,
    done,
    sems,
):
    chan = x_ref.shape[2]
    img = lax.axis_index("img")
    bal = lax.axis_index("bal")
    img_even = img % 2 == 0
    bal_even = bal % 2 == 0

    groups = mean_ref.shape[1]
    group_of = lax.broadcasted_iota(jnp.int32, (groups, chan), 1) // (chan // groups)
    spread = lax.broadcasted_iota(jnp.int32, (groups, chan), 0) == group_of
    square = (groups, groups)
    diagonal = lax.broadcasted_iota(jnp.int32, square, 0) == lax.broadcasted_iota(jnp.int32, square, 1)

    def per_channel(ref):
        column = jnp.sum(jnp.where(diagonal, ref[...], 0.0), axis=1, keepdims=True)
        return jnp.sum(jnp.where(spread, column, 0.0), axis=0, keepdims=True)

    mean = per_channel(mean_ref)
    rstd = per_channel(rstd_ref)
    gain = gain_ref[...]
    shift = shift_ref[...]

    scale = 0.5 * rstd * gain
    offset = 0.5 * shift - mean * scale

    def activate(cells):
        v = cells * scale + offset
        return v * jnp.tanh(v) + v

    side = ROWS + 4
    lines = [x_ref[r] for r in range(ROWS)]
    lines = [jnp.where(img_even, row_z[r], row_core[0, r]) for r in range(2)] + lines
    lines += [jnp.where(img_even, row_core[1, r], row_z[r]) for r in range(2)]
    for r, line in enumerate(lines):
        left = jnp.where(bal_even, col_odd[r], col_even[0, r])
        right = jnp.where(bal_even, col_even[1, r], col_odd[r])
        at = r * PITCH
        act[at : at + 2] = left.astype(F32)
        act[at + 2 : at + 2 + COLS] = line.astype(F32)
        act[at + 2 + COLS : at + PITCH] = right.astype(F32)
    cell = lax.broadcasted_iota(jnp.int32, (PITCH, 1), 0)
    col = bal * COLS - 2 + cell
    col_ok = (col >= 0) & (col < full_cols)
    for r in range(side):
        row = img * ROWS - 2 + r
        ok = col_ok & ((row >= 0) & (row < full_rows))
        at = slice(r * PITCH, (r + 1) * PITCH)
        act[at] = jnp.where(ok, activate(act[at]), 0.0)
    total = side * PITCH
    act[total:] = jnp.zeros((act.shape[0] - total, chan), F32)

    for d in range(3):
        taps[:, d * chan : (d + 1) * chan] = act[d : d + total].astype(BF16)

    inner = (ROWS + 2) * PITCH
    cell = lax.broadcasted_iota(jnp.int32, (inner, 1), 0)
    row = img * ROWS - 1 + cell // PITCH
    col = bal * COLS - 1 + cell % PITCH
    ok = (row >= 0) & (row < full_rows) & (col >= 0) & (col < full_cols)
    parts = [slice(n, n + SPLIT) for n in range(0, chan, SPLIT)]

    for part in parts:
        h = b1_ref[:, part]
        for d in range(3):
            h = h + jnp.dot(
                taps[d * PITCH : d * PITCH + inner], w1_ref[d, :, part], preferred_element_type=F32
            )
        hid[:, part] = jnp.where(ok, h, 0.0).astype(BF16)

    cell = lax.broadcasted_iota(jnp.int32, (2 * COLS, TC), 0)
    own = cell // (2 * TS) == lax.broadcasted_iota(jnp.int32, (2 * COLS, TC), 1)
    live = [
        jnp.max(jnp.where(own, dest_ref[i : i + 1], -1), axis=1, keepdims=True) >= 0
        for i in range(TR)
    ]
    span = ROWS * PITCH
    met = ((0, PITCH + span), (PITCH, PITCH + span), (PITCH, 2 * PITCH + span))

    within = slice(MARGIN, MARGIN + 2 * COLS)
    copies = []
    for n, part in enumerate(parts):
        lanes = range(part.start // LANES, part.stop // LANES)
        bias = b2_ref[:, part]

        def scatter(side, p, q, shift, sums):
            at = pl.ds(MARGIN - 2 * shift + q, PITCH, stride=2)
            for r in range(ROWS):
                cells = sums[r * PITCH : (r + 1) * PITCH]
                for lane, k in enumerate(lanes):
                    wide[side, k, 2 * r + p, at] = cells[:, lane * LANES : (lane + 1) * LANES]

        by_row = []
        for dx in range(3):
            first, mid, last = (
                jnp.dot(hid[a:b], w2_ref[dy, dx, :, part], preferred_element_type=F32)
                for dy, (a, b) in enumerate(met)
            )
            if dx == 1:
                mid = mid + bias
            by_row.append((first[:span] + (mid + last[:span]), (first[PITCH:] + mid) + last[PITCH:]))
            for p in range(2):
                if dx == 0:
                    scatter(0, p, 0, 0, by_row[0][p])
                elif dx == 1:
                    scatter(0, p, 1, 1, by_row[0][p] + by_row[1][p])
                else:
                    scatter(1, p, 0, 1, by_row[1][p] + by_row[2][p])
                    scatter(1, p, 1, 2, by_row[2][p])
        for row in range(2 * ROWS):
            for k in lanes:
                cells = wide[0, k, row, within] + wide[1, k, row, within]
                lane = slice(k * LANES, (k + 1) * LANES)
                done[row, :, lane] = jnp.where(live[row // (2 * TS)], cells, 0.0).astype(BF16)
            if (row + 1) % BATCH == 0:
                at = (slice(row + 1 - BATCH, row + 1), slice(None), part)
                copy = pltpu.make_async_copy(done.at[at], o_ref.at[at], sems.at[len(copies)])
                copy.start()
                copies.append(copy)
    for copy in copies:
        copy.wait()


def run_block(full_rows, full_cols, *args):
    chan = args[0].shape[2]
    vmem = pl.BlockSpec(memory_space=pltpu.VMEM)
    side = ROWS + 4
    inner = (ROWS + 2) * PITCH
    return pl.pallas_call(
        functools.partial(block_kernel, full_rows, full_cols),
        out_shape=jax.ShapeDtypeStruct((2 * ROWS, 2 * COLS, chan), BF16),
        in_specs=[vmem] * 14,
        out_specs=pl.BlockSpec(memory_space=pltpu.HBM),
        scratch_shapes=[
            pltpu.VMEM((side * PITCH + 8, chan), F32),
            pltpu.VMEM((side * PITCH, 3 * chan), BF16),
            pltpu.VMEM((inner, chan), BF16),
            pltpu.VMEM((2, chan // LANES, 2 * ROWS, MARGIN + 2 * PITCH, LANES), F32),
            pltpu.VMEM((2 * ROWS, 2 * COLS, chan), BF16),
            pltpu.SemaphoreType.DMA((chan // SPLIT * 2 * ROWS // BATCH,)),
        ],
        compiler_params=pltpu.CompilerParams(vmem_limit_bytes=36 * 2**20),
        cost_estimate=pl.CostEstimate(
            flops=2_300_000_000, bytes_accessed=14_000_000, transcendentals=131_072
        ),
        name="decode_block",
    )(*args)


def shards(
    latent,
    gn_mean,
    gn_rstd,
    gn_gain,
    gn_shift,
    conv1_kernel,
    conv1_bias,
    conv2_kernel,
    conv2_bias,
    tile_dest,
):
    chan = latent.shape[2]
    full_rows = latent.shape[0] * lax.axis_size("img")
    full_cols = latent.shape[1] * lax.axis_size("bal")
    mesh_axes = ("img", "bal")
    core_pairs, even_pairs = pair_groups(lax.axis_size("img"), lax.axis_size("bal"))
    edge_core, edge_z = row_edges(latent)
    row_z = lax.ppermute(edge_z, "img", swaps(lax.axis_size("img"), 1))
    edge_core = keep(edge_core, conv1_kernel, conv2_kernel)
    row_core = lax.all_gather(edge_core, mesh_axes, axis_index_groups=core_pairs)
    edge_odd, edge_even = column_edges(latent, row_z, row_core)
    col_odd = lax.ppermute(edge_odd, "bal", swaps(lax.axis_size("bal"), 1))
    col_even = lax.all_gather(edge_even, mesh_axes, axis_index_groups=even_pairs)
    return run_block(
        full_rows,
        full_cols,
        latent,
        row_z,
        row_core,
        col_odd,
        col_even,
        gn_mean.reshape(1, -1),
        gn_rstd.reshape(1, -1),
        gn_gain.reshape(1, chan),
        gn_shift.reshape(1, chan),
        conv1_kernel.reshape(3, 3 * chan, -1),
        conv1_bias.reshape(1, -1),
        conv2_kernel,
        conv2_bias.reshape(1, -1),
        tile_dest,
    )


def solution(mesh):
    placed = (P("img", "bal", None), P(), P(), P(), P(), P(), P(), P(), P(), P("img", "bal"))
    return jax.shard_map(
        shards, mesh=mesh, in_specs=placed, out_specs=P("img", "bal", None), check_vma=False
    )
```

```python
import functools

import jax
import jax.numpy as jnp
from jax import lax
from jax.experimental import pallas as pl
from jax.experimental.pallas import tpu as pltpu
from jax.sharding import PartitionSpec as P

TS = 3
TR = 4
TC = 4
ROWS = TR * TS
COLS = TC * TS
LANES = 128
SPLIT = 256
BATCH = 12
MARGIN = 8
PITCH = 16
F32 = jnp.float32
BF16 = jnp.bfloat16


def swaps(count, first):
    pairs = []
    for i in range(first, count - 1, 2):
        pairs += [(i, i + 1), (i + 1, i)]
    return pairs


def pair_groups(rows, cols):
    img = [[i * cols + j, (i + 1) * cols + j] for i in range(0, rows, 2) for j in range(cols)]
    bal = [[i * cols + j, i * cols + j + 1] for i in range(rows) for j in range(0, cols, 2)]
    return img, bal


def rows_kernel(x_hbm, core_ref, z_ref, sems):
    img_even = lax.axis_index("img") % 2 == 0
    last = x_hbm.shape[0] - 2
    core_at = jnp.where(img_even, last, 0)
    copies = [
        pltpu.make_async_copy(source, ref, sems.at[n])
        for n, (source, ref) in enumerate(
            (
                (x_hbm.at[pl.ds(last - core_at, 2)], z_ref),
                (x_hbm.at[pl.ds(core_at, 2)], core_ref),
            )
        )
    ]
    for copy in copies:
        copy.start()
    for copy in copies:
        copy.wait()


def row_edges(x):
    vmem = pl.BlockSpec(memory_space=pltpu.VMEM)
    edge = jax.ShapeDtypeStruct((2,) + x.shape[1:], BF16)
    return pl.pallas_call(
        rows_kernel,
        out_shape=(edge, edge),
        in_specs=[pl.BlockSpec(memory_space=pltpu.HBM)],
        out_specs=(vmem, vmem),
        scratch_shapes=[pltpu.SemaphoreType.DMA((2,))],
        compiler_params=pltpu.CompilerParams(vmem_limit_bytes=4 * 2**20),
        cost_estimate=pl.CostEstimate(flops=0, bytes_accessed=500_000, transcendentals=0),
        name="row_edges",
    )(pltpu.with_memory_space_constraint(x, pltpu.HBM))


def keep_kernel(edge_ref, *refs):
    refs[-1][...] = edge_ref[...]


def keep(edge, w1, w2):
    vmem = pl.BlockSpec(memory_space=pltpu.VMEM)
    return pl.pallas_call(
        keep_kernel,
        out_shape=jax.ShapeDtypeStruct(edge.shape, edge.dtype),
        in_specs=[vmem] + [pl.BlockSpec(memory_space=pltpu.HBM)] * 6,
        out_specs=vmem,
        compiler_params=pltpu.CompilerParams(vmem_limit_bytes=4 * 2**20),
        name="keep",
    )(edge, *(pltpu.with_memory_space_constraint(a, pltpu.HBM) for a in (w1, w2) * 3))


def columns_kernel(x_ref, row_z, row_core, odd_ref, even_ref):
    img_even = lax.axis_index("img") % 2 == 0
    bal_even = lax.axis_index("bal") % 2 == 0
    last = x_ref.shape[1]

    def put(row, cells):
        head, tail = cells[0:2], cells[last - 2 : last]
        odd_ref[row] = jnp.where(bal_even, head, tail)
        even_ref[row] = jnp.where(bal_even, tail, head)

    for r in range(2):
        put(r, jnp.where(img_even, row_z[r], row_core[0, r]))
        put(r + 2 + ROWS, jnp.where(img_even, row_core[1, r], row_z[r]))
    for r in range(ROWS):
        put(r + 2, x_ref[r])


def column_edges(x, row_z, row_core):
    vmem = pl.BlockSpec(memory_space=pltpu.VMEM)
    edge = jax.ShapeDtypeStruct((ROWS + 4, 2, x.shape[2]), BF16)
    return pl.pallas_call(
        columns_kernel,
        out_shape=(edge, edge),
        in_specs=[vmem] * 3,
        out_specs=(vmem, vmem),
        compiler_params=pltpu.CompilerParams(vmem_limit_bytes=4 * 2**20),
        cost_estimate=pl.CostEstimate(flops=0, bytes_accessed=30_000_000, transcendentals=0),
        name="column_edges",
    )(x, row_z, row_core)


def block_kernel(
    full_rows,
    full_cols,
    x_ref,
    row_z,
    row_core,
    col_odd,
    col_even,
    mean_ref,
    rstd_ref,
    gain_ref,
    shift_ref,
    w1_ref,
    b1_ref,
    w2_ref,
    b2_ref,
    dest_ref,
    o_ref,
    act,
    taps,
    hid,
    wide,
    done,
    sems,
):
    chan = x_ref.shape[2]
    img = lax.axis_index("img")
    bal = lax.axis_index("bal")
    img_even = img % 2 == 0
    bal_even = bal % 2 == 0

    groups = mean_ref.shape[1]
    group_of = lax.broadcasted_iota(jnp.int32, (groups, chan), 1) // (chan // groups)
    spread = lax.broadcasted_iota(jnp.int32, (groups, chan), 0) == group_of
    square = (groups, groups)
    diagonal = lax.broadcasted_iota(jnp.int32, square, 0) == lax.broadcasted_iota(jnp.int32, square, 1)

    def per_channel(ref):
        column = jnp.sum(jnp.where(diagonal, ref[...], 0.0), axis=1, keepdims=True)
        return jnp.sum(jnp.where(spread, column, 0.0), axis=0, keepdims=True)

    mean = per_channel(mean_ref)
    rstd = per_channel(rstd_ref)
    gain = gain_ref[...]
    shift = shift_ref[...]

    scale = 0.5 * rstd * gain
    offset = 0.5 * shift - mean * scale

    def activate(cells):
        v = cells * scale + offset
        return v * jnp.tanh(v) + v

    side = ROWS + 4
    lines = [x_ref[r] for r in range(ROWS)]
    lines = [jnp.where(img_even, row_z[r], row_core[0, r]) for r in range(2)] + lines
    lines += [jnp.where(img_even, row_core[1, r], row_z[r]) for r in range(2)]
    cell = lax.broadcasted_iota(jnp.int32, (PITCH, 1), 0)
    col = bal * COLS - 2 + cell
    col_ok = (col >= 0) & (col < full_cols)
    for r, line in enumerate(lines):
        left = jnp.where(bal_even, col_odd[r], col_even[0, r])
        right = jnp.where(bal_even, col_even[1, r], col_odd[r])
        row = img * ROWS - 2 + r
        ok = col_ok & ((row >= 0) & (row < full_rows))
        cells = jnp.concatenate([c.astype(F32) for c in (left, line, right)], axis=0)
        act[r * PITCH : (r + 1) * PITCH] = jnp.where(ok, activate(cells), 0.0)
    total = side * PITCH
    act[total:] = jnp.zeros((act.shape[0] - total, chan), F32)

    for d in range(3):
        taps[:, d * chan : (d + 1) * chan] = act[d : d + total].astype(BF16)

    inner = (ROWS + 2) * PITCH
    cell = lax.broadcasted_iota(jnp.int32, (inner, 1), 0)
    row = img * ROWS - 1 + cell // PITCH
    col = bal * COLS - 1 + cell % PITCH
    ok = (row >= 0) & (row < full_rows) & (col >= 0) & (col < full_cols)
    parts = [slice(n, n + SPLIT) for n in range(0, chan, SPLIT)]

    for part in parts:
        h = b1_ref[:, part]
        for d in range(3):
            h = h + jnp.dot(
                taps[d * PITCH : d * PITCH + inner], w1_ref[d, :, part], preferred_element_type=F32
            )
        hid[:, part] = jnp.where(ok, h, 0.0).astype(BF16)

    cell = lax.broadcasted_iota(jnp.int32, (2 * COLS, TC), 0)
    own = cell // (2 * TS) == lax.broadcasted_iota(jnp.int32, (2 * COLS, TC), 1)
    live = [
        jnp.max(jnp.where(own, dest_ref[i : i + 1], -1), axis=1, keepdims=True) >= 0
        for i in range(TR)
    ]
    span = ROWS * PITCH
    met = ((0, PITCH + span), (PITCH, PITCH + span), (PITCH, 2 * PITCH + span))

    within = slice(MARGIN, MARGIN + 2 * COLS)
    copies = []
    for n, part in enumerate(parts):
        lanes = range(part.start // LANES, part.stop // LANES)
        bias = b2_ref[:, part]

        def scatter(side, p, q, shift, sums):
            at = pl.ds(MARGIN - 2 * shift + q, PITCH, stride=2)
            for r in range(ROWS):
                cells = sums[r * PITCH : (r + 1) * PITCH]
                for lane, k in enumerate(lanes):
                    wide[side, k, 2 * r + p, at] = cells[:, lane * LANES : (lane + 1) * LANES]

        by_row = []
        for dx in range(3):
            first, mid, last = (
                jnp.dot(hid[a:b], w2_ref[dy, dx, :, part], preferred_element_type=F32)
                for dy, (a, b) in enumerate(met)
            )
            if dx == 1:
                mid = mid + bias
            by_row.append((first[:span] + (mid + last[:span]), (first[PITCH:] + mid) + last[PITCH:]))
            for p in range(2):
                if dx == 0:
                    scatter(0, p, 0, 0, by_row[0][p])
                elif dx == 1:
                    scatter(0, p, 1, 1, by_row[0][p] + by_row[1][p])
                else:
                    scatter(1, p, 0, 1, by_row[1][p] + by_row[2][p])
                    scatter(1, p, 1, 2, by_row[2][p])
        for row in range(2 * ROWS):
            for k in lanes:
                cells = wide[0, k, row, within] + wide[1, k, row, within]
                lane = slice(k * LANES, (k + 1) * LANES)
                done[row, :, lane] = jnp.where(live[row // (2 * TS)], cells, 0.0).astype(BF16)
            if (row + 1) % BATCH == 0:
                at = (slice(row + 1 - BATCH, row + 1), slice(None), part)
                copy = pltpu.make_async_copy(done.at[at], o_ref.at[at], sems.at[len(copies)])
                copy.start()
                copies.append(copy)
    for copy in copies:
        copy.wait()


def run_block(full_rows, full_cols, *args):
    chan = args[0].shape[2]
    vmem = pl.BlockSpec(memory_space=pltpu.VMEM)
    side = ROWS + 4
    inner = (ROWS + 2) * PITCH
    return pl.pallas_call(
        functools.partial(block_kernel, full_rows, full_cols),
        out_shape=jax.ShapeDtypeStruct((2 * ROWS, 2 * COLS, chan), BF16),
        in_specs=[vmem] * 14,
        out_specs=pl.BlockSpec(memory_space=pltpu.HBM),
        scratch_shapes=[
            pltpu.VMEM((side * PITCH + 8, chan), F32),
            pltpu.VMEM((side * PITCH, 3 * chan), BF16),
            pltpu.VMEM((inner, chan), BF16),
            pltpu.VMEM((2, chan // LANES, 2 * ROWS, MARGIN + 2 * PITCH, LANES), F32),
            pltpu.VMEM((2 * ROWS, 2 * COLS, chan), BF16),
            pltpu.SemaphoreType.DMA((chan // SPLIT * 2 * ROWS // BATCH,)),
        ],
        compiler_params=pltpu.CompilerParams(vmem_limit_bytes=36 * 2**20),
        cost_estimate=pl.CostEstimate(
            flops=2_300_000_000, bytes_accessed=14_000_000, transcendentals=131_072
        ),
        name="decode_block",
    )(*args)


def shards(
    latent,
    gn_mean,
    gn_rstd,
    gn_gain,
    gn_shift,
    conv1_kernel,
    conv1_bias,
    conv2_kernel,
    conv2_bias,
    tile_dest,
):
    chan = latent.shape[2]
    full_rows = latent.shape[0] * lax.axis_size("img")
    full_cols = latent.shape[1] * lax.axis_size("bal")
    mesh_axes = ("img", "bal")
    core_pairs, even_pairs = pair_groups(lax.axis_size("img"), lax.axis_size("bal"))
    edge_core, edge_z = row_edges(latent)
    row_z = lax.ppermute(edge_z, "img", swaps(lax.axis_size("img"), 1))
    edge_core = keep(edge_core, conv1_kernel, conv2_kernel)
    row_core = lax.all_gather(edge_core, mesh_axes, axis_index_groups=core_pairs)
    edge_odd, edge_even = column_edges(latent, row_z, row_core)
    col_odd = lax.ppermute(edge_odd, "bal", swaps(lax.axis_size("bal"), 1))
    col_even = lax.all_gather(edge_even, mesh_axes, axis_index_groups=even_pairs)
    return run_block(
        full_rows,
        full_cols,
        latent,
        row_z,
        row_core,
        col_odd,
        col_even,
        gn_mean.reshape(1, -1),
        gn_rstd.reshape(1, -1),
        gn_gain.reshape(1, chan),
        gn_shift.reshape(1, chan),
        conv1_kernel.reshape(3, 3 * chan, -1),
        conv1_bias.reshape(1, -1),
        conv2_kernel,
        conv2_bias.reshape(1, -1),
        tile_dest,
    )


def solution(mesh):
    placed = (P("img", "bal", None), P(), P(), P(), P(), P(), P(), P(), P(), P("img", "bal"))
    return jax.shard_map(
        shards, mesh=mesh, in_specs=placed, out_specs=P("img", "bal", None), check_vma=False
    )
```
